32 devices in a mesh: group: 2 (over y), area: 4 (over z), region: 2 (over x), scen: 2 (over core).
Axes of the slice: x: 2, y: 2, z: 4, core: 2. Of those that a mesh axis runs over, the one named last changes fastest.
Arguments:
- kkt_inverse: float32 [8, 256, 256], P(('area', 'region')), may hold values from -1 to 1
- scen_load: float32 [8, 256, 1024], P(('area', 'region'), None, ('group', 'scen')), parts along dimension 2, may hold values from -12 to 12
- capacity: float32 [8, 256], P(('area', 'region')), may hold values from 0.3 to 3
- pair_active: int32 [8, 6], P(('area', 'region')), may hold values from 0 to 1, as said below
- tie_counts: int32 [8, 6], P(('area', 'region')), may hold values from 64 to 384, as said below
- line_index: int32 [8, 6, 384], P(('area', 'region')), may hold values from 0 to 127
- area_zone: int32 [8], P(('area', 'region')), may hold values from 0 to 3
Outputs:
- injection: float32 [8, 256, 1024], P(('area', 'region'), None, ('group', 'scen')), parts along dimension 2
- tie_flow: float32 [8, 6, 384, 1024], P(('area', 'region'), None, None, ('group', 'scen')), parts along dimension 3
- zone_prices: float32 [8, 1024], P('region', ('group', 'scen')), parts along dimension 1
The draws below stay inside these ranges and needn't reach their ends.
There are 2 independent parts, one for each index of `group`. The reference program is written for one: setup_inputs(seed, part) draws one part's arguments, and reference() takes and returns one part's arrays. A program takes and returns all parts, laid end to end along the dimension named above; an argument that names none is the same for every part. Nothing has to cross between parts.
Inputs may be any that keep to these rules, and one draw needn't show every extreme that they name: `pair_active`: for every area and slot, the neighbour that the slot points to holds the same value on the slot that points back; the pair with 384 lines and one with 64 lines are always present. `tie_counts`: equal on both ends of a pair, as for pair_active.
All inputs are finite; a program needn't handle non-finite values.
Results may differ from the reference program's by a relative error of at most 0.0001.
Values sent between devices are 32-bit elements; how exact they have to be, the bound alone decides.
No kernel may reach another device: no remote copies, remote signals or barrier semaphores. Data moves between devices by JAX's collectives and lax.ppermute only.
A program may use at most 64 MiB of HBM per device.

```python
import math
import jax
import jax.numpy as jnp
from jax import lax

NB = 256
NBD = 128
SLOTS = 6
MAXL = 384
MINL = 64
ZONES = 4
INNER = 24
ROUNDS = 2
SCEN = 512
AREAS = 8
N_AREA = 4
N_REGION = 2


def pair_tables(key):
    ident = jnp.arange(AREAS, dtype=jnp.int32)
    position = ident // N_REGION
    region_pos = ident % N_REGION
    actives = []
    numbers = []
    for slot_pair, moves in enumerate(((1, 0), (2, 0), (0, 1))):
        live = (jax.random.randint(jax.random.fold_in(key, 40 + slot_pair), (AREAS,), 0, 4) > 0).astype(jnp.int32)
        number = jax.random.randint(jax.random.fold_in(key, 50 + slot_pair), (AREAS,), MINL, MAXL + 1).astype(jnp.int32)
        if slot_pair == 0:
            live = live.at[0].set(1)
            number = number.at[0].set(MAXL)
        if slot_pair == 1:
            live = live.at[0].set(1)
            number = number.at[0].set(MINL)
        source = (position - moves[0]) % N_AREA * N_REGION + (region_pos - moves[1]) % N_REGION
        actives += [live, live[source]]
        numbers += [number, number[source]]
    return (jnp.stack(actives, axis=1), jnp.stack(numbers, axis=1))


def draw_pair_active(key, part):
    return pair_tables(key)[0]


def draw_tie_counts(key, part):
    return pair_tables(key)[1]


def draw_kkt_inverse(key, part):
    key = jax.random.fold_in(key, 5)
    diagonal = 0.4 * jax.random.uniform(jax.random.fold_in(key, 1), (AREAS, NB), jnp.float32, 0.8, 1.2)
    spread = jnp.clip(jax.random.normal(jax.random.fold_in(key, 2), (AREAS, NB, NB), jnp.float32), -4.0, 4.0)
    spread = spread * (0.25 / NB ** 0.5)
    unit = jnp.eye(NB, dtype=jnp.float32)
    return spread * (1.0 - unit)[None] + unit[None] * diagonal[:, :, None]


def draw_scen_load(key, part):
    key = jax.random.fold_in(key, 11)
    area_ramp = 1.0 + 2.0 * jnp.arange(AREAS, dtype=jnp.float32)[:, None, None] / AREAS
    noise_part = jnp.clip(jax.random.normal(jax.random.fold_in(key, 1), (AREAS, NB, SCEN), jnp.float32), -4.0, 4.0)
    return area_ramp * noise_part


def with_ends(values, stream_key, smallest, top_value):
    longest = values.shape.index(max(values.shape))
    spots = []
    for shift in (0, 1):
        where = [jax.random.randint(jax.random.fold_in(stream_key, axis), (), 0, length) for axis, length in enumerate(values.shape)]
        where[longest] = (where[longest] + shift) % values.shape[longest]
        spots.append(tuple(where))
    return values.at[spots[0]].set(smallest).at[spots[1]].set(top_value)


def shard_levels(own_key, extent, pieces, low, top_value):
    level, own = 1.0, jax.random.fold_in(own_key, 6)
    for axis_at, shards_of in pieces:
        draws = jnp.exp(jax.random.uniform(jax.random.fold_in(own, axis_at), (shards_of,), jnp.float32, low / len(pieces), top_value / len(pieces)))
        level = level * jnp.repeat(draws, extent[axis_at] // shards_of).reshape([-1 if axis == axis_at else 1 for axis in range(len(extent))])
    return level


def setup_inputs(seed: int = 0, part: int = 0) -> dict:
    keys = jax.random.split(jax.random.key(seed), 8)
    part_splits = jax.random.split(jax.random.fold_in(keys[7], part), 8)
    kkt_inverse = draw_kkt_inverse(jax.random.fold_in(keys[7], 71), part)
    scen_load = draw_scen_load(jax.random.fold_in(jax.random.fold_in(keys[7], part), 71), part)
    capacity = jnp.clip(jnp.exp(math.log(3.0) - 2.3025851 * jax.random.uniform(keys[2], (AREAS, NB), jnp.float32) ** shard_levels(keys[2], (AREAS, NB), ((0, 8),), -0.2, 0.2)), 0.3, 3.0)
    pair_active = draw_pair_active(jax.random.fold_in(keys[7], 71), part)
    tie_counts = draw_tie_counts(jax.random.fold_in(keys[7], 71), part)
    line_index = with_ends(jax.random.randint(keys[5], (AREAS, SLOTS, MAXL), 0, NBD), jax.random.fold_in(keys[5], 1), 0, NBD - 1).astype(jnp.int32)
    area_zone = with_ends(jax.random.randint(keys[6], (AREAS,), 0, ZONES), jax.random.fold_in(keys[6], 1), 0, ZONES - 1).astype(jnp.int32)
    return dict(kkt_inverse=kkt_inverse, scen_load=scen_load, capacity=capacity, pair_active=pair_active, tie_counts=tie_counts, line_index=line_index, area_zone=area_zone)


PENALTY = 1.0
ZONE_GAIN = 0.004
SYSTEM_GAIN = 0.001


def slot_tables():
    area_moves = jnp.array([1, -1, 2, -2, 0, 0], jnp.int32)
    region_moves = jnp.array([0, 0, 0, 0, 1, -1], jnp.int32)
    reverse = jnp.array([1, 0, 3, 2, 5, 4], jnp.int32)
    side_sign = jnp.array([1.0, -1.0, 1.0, -1.0, 1.0, -1.0], jnp.float32)
    return area_moves, region_moves, reverse, side_sign


def reference(kkt_inverse, scen_load, capacity, pair_active, tie_counts, line_index, area_zone):
    area_count = scen_load.shape[0]
    scen_count = scen_load.shape[2]
    area_moves, region_moves, reverse, side_sign = slot_tables()
    ident = jnp.arange(area_count, dtype=jnp.int32)
    position = ident // N_REGION
    region_pos = ident % N_REGION
    peer = ((position[:, None] + area_moves[None, :]) % N_AREA) * N_REGION + (region_pos[:, None] + region_moves[None, :]) % N_REGION
    positions = jnp.arange(MAXL, dtype=jnp.int32)
    live_mask = ((pair_active[:, :, None] > 0) & (positions[None, None, :] < tie_counts[:, :, None])).astype(jnp.float32)[..., None]
    signs = side_sign[None, :, None, None]
    flat_index = line_index.reshape(area_count, SLOTS * MAXL)
    zone_row = region_pos * ZONES + area_zone
    zone_price = jnp.zeros((N_REGION * ZONES, scen_count), jnp.float32)
    system_price = jnp.zeros((scen_count,), jnp.float32)
    tie_flow = jnp.zeros((area_count, SLOTS, MAXL, scen_count), jnp.float32)
    duals = jnp.zeros((area_count, SLOTS, MAXL, scen_count), jnp.float32)
    clipped = jnp.zeros((area_count, NB, scen_count), jnp.float32)
    scaled = jnp.zeros((area_count, NB, scen_count), jnp.float32)
    solution = jnp.zeros((area_count, NB, scen_count), jnp.float32)
    limits = capacity[:, :, None]

    def scatter_rows(rows_index, values):
        return jnp.zeros((NB, scen_count), jnp.float32).at[rows_index].add(values)

    def pick_rows(field, rows_index):
        return field[rows_index]

    for round_index in range(ROUNDS):
        area_price = zone_price[zone_row] + system_price[None, :]
        coupling_term = (PENALTY * signs * (tie_flow - duals)).reshape(area_count, SLOTS * MAXL, scen_count)
        coupling = jax.vmap(scatter_rows)(flat_index, coupling_term)
        linear = scen_load - area_price[:, None, :] + coupling

        def box_sweep(step_index, state):
            solution, clipped, scaled = state
            solution = jnp.einsum("aij,ajs->ais", kkt_inverse, linear + clipped - scaled, precision=lax.Precision.HIGHEST)
            clipped = jnp.clip(solution + scaled, -limits, limits)
            scaled = scaled + solution - clipped
            return solution, clipped, scaled

        solution, clipped, scaled = lax.fori_loop(0, INNER, box_sweep, (solution, clipped, scaled))
        own_view = signs * jax.vmap(pick_rows)(solution, flat_index).reshape(area_count, SLOTS, MAXL, scen_count)
        own_offer = own_view + duals
        peer_offer = own_offer[peer, reverse[None, :]]
        tie_flow = live_mask * (0.5 * (own_offer + peer_offer))
        duals = live_mask * (own_offer - tie_flow)
        mismatch = jnp.sum(solution, axis=1) - jnp.sum(signs * tie_flow, axis=(1, 2))
        zone_sum = jax.ops.segment_sum(mismatch, zone_row, num_segments=N_REGION * ZONES)
        system_total = jnp.sum(mismatch, axis=0)
        zone_price = zone_price + ZONE_GAIN * zone_sum
        system_price = system_price + SYSTEM_GAIN * system_total
    return solution, tie_flow, zone_price + system_price[None, :]
```

```python
import functools

import jax
import jax.numpy as jnp
from jax import lax
from jax.experimental import pallas as pl
from jax.experimental.pallas import tpu as pltpu
from jax.sharding import PartitionSpec as P

ZONES = 4
INNER = 24
BOUNDARY = 128
LANES = 128
ZONE_GAIN = 0.004
SYSTEM_GAIN = 0.001
SLOTS = (
    ("area", 1, 1),
    ("area", -1, 0),
    ("area", 2, 3),
    ("area", -2, 2),
    ("region", 1, 5),
    ("region", -1, 4),
)
SIGNS = (1.0, -1.0, 1.0, -1.0, 1.0, -1.0)
CHAIN_ROWS = 64

F32 = jnp.float32
BF16 = jnp.bfloat16
VMEM = pl.BlockSpec(memory_space=pltpu.VMEM)
SMEM = pl.BlockSpec(memory_space=pltpu.SMEM)
PARAMS = pltpu.CompilerParams(vmem_limit_bytes=40 * 2**20)


def dot(a, b):
    return jnp.dot(a, b, preferred_element_type=F32)


def dot_nt(a, b):
    return lax.dot_general(a, b, (((1,), (1,)), ((), ())), preferred_element_type=F32)


def halves(x):
    high = x.astype(BF16)
    return high, (x - high.astype(F32)).astype(BF16)


def thirds(x):
    high = x.astype(BF16)
    rest = x - high.astype(F32)
    middle = rest.astype(BF16)
    return high, middle, (rest - middle.astype(F32)).astype(BF16)


def product(x, kh_ref, kl_ref):
    high, low = halves(x)
    return dot(high, kh_ref[...]) + dot(low, kh_ref[...]) + dot(high, kl_ref[...])


def run_sweeps(states, lin_ref, limits, kh_ref, kl_ref, count):
    injections = [None] * len(states)
    for _ in range(count):
        for i in range(len(states)):
            lin = lin_ref[pl.ds(i * CHAIN_ROWS, CHAIN_ROWS), :]
            v = states[i]
            if v is None:
                injections[i] = product(lin, kh_ref, kl_ref)
                states[i] = injections[i]
                continue
            clipped = jnp.clip(v, -limits, limits)
            over = v - clipped
            injections[i] = product(lin + (clipped - over), kh_ref, kl_ref)
            states[i] = injections[i] + over
    return injections, states


def first_kernel(k_ref, load_ref, cap_ref, idx_ref, edge_ref, rest_ref, v_ref, lin_ref, kh_ref, kl_ref):
    scens = lin_ref.shape[0]
    high, low = halves(k_ref[0].T)
    kh_ref[...] = high
    kl_ref[...] = low
    lin_ref[...] = load_ref[0].T
    slots, lines = idx_ref.shape[1:]
    pieces = lines // LANES
    edge_ref[pl.ds(scens, edge_ref.shape[0] - scens), :] = jnp.zeros((edge_ref.shape[0] - scens, LANES), F32)
    for p in range(slots):
        for j in range(pieces):
            row = idx_ref[0, pl.ds(p, 1), pl.ds(j * LANES, LANES)]
            edge_ref[pl.ds(scens + p * pieces + j, 1), :] = row.astype(F32)
    injections, states = run_sweeps([None] * (scens // CHAIN_ROWS), lin_ref, cap_ref[...], kh_ref, kl_ref, INNER)
    for i, (x, v) in enumerate(zip(injections, states)):
        rows = pl.ds(i * CHAIN_ROWS, CHAIN_ROWS)
        edge_ref[rows, :] = x[:, :BOUNDARY]
        rest_ref[rows, :] = x[:, BOUNDARY:]
        v_ref[rows, :] = v


def live_lines(active_ref, count_ref, p):
    return jnp.where(active_ref[0, p] > 0, count_ref[0, p], 0)


def peer_ident(p, areas, regions):
    axis, move, _ = SLOTS[p]
    a = lax.axis_index("area")
    r = lax.axis_index("region")
    if axis == "area":
        a = lax.rem(a + (move % areas), areas)
    else:
        r = lax.rem(r + (move % regions), regions)
    return a * regions + r


def weighted_sums(weights, edge, rest):
    wh, wl = halves(weights)
    eh, em, el = thirds(edge)
    out = dot_nt(wh[:, :BOUNDARY], eh) + dot_nt(wh[:, :BOUNDARY], em) + dot_nt(wh[:, :BOUNDARY], el)
    out = out + dot_nt(wl[:, :BOUNDARY], eh) + dot_nt(wl[:, :BOUNDARY], em)
    for part in thirds(rest):
        out = out + dot_nt(wh[:, BOUNDARY:], part)
    return out


def share_kernel(
    areas, regions, active_ref, count_ref, zone_ref, edge_ref, rest_ref, idx_ref, share_ref, own_ref, weight_ref
):
    total = areas * regions
    rows = share_ref.shape[0]
    scens = rest_ref.shape[0]
    slots, lines = idx_ref.shape[1:]
    me = lax.axis_index("area") * regions + lax.axis_index("region")
    row_id = lax.broadcasted_iota(jnp.int32, (rows, lines), 0)
    line_id = lax.broadcasted_iota(jnp.int32, (1, lines), 1)
    bus_id = lax.broadcasted_iota(jnp.int32, (BOUNDARY, lines), 0)
    weights = jnp.zeros((rows, BOUNDARY), F32)
    for p in range(slots):
        live = line_id < live_lines(active_ref, count_ref, p)
        onehot = jnp.where((bus_id == idx_ref[0, pl.ds(p, 1), :]) & live, 1.0, 0.0).astype(BF16)
        own_ref[:, pl.ds(p * lines, lines)] = onehot
        peer = peer_ident(p, areas, regions)
        coefficient = jnp.where(row_id == peer, 0.5, 0.0) - jnp.where(row_id == me, 0.5, 0.0)
        weights = weights + dot_nt(coefficient.astype(BF16), onehot)
    mine = jnp.where(lax.broadcasted_iota(jnp.int32, (rows, BOUNDARY), 0) == me, 1.0, 0.0)
    weights = jnp.concatenate([weights + mine, mine], axis=1)
    weight_ref[...] = weights
    sums = weighted_sums(weights, edge_ref[pl.ds(0, scens), :], rest_ref[...])
    scen_row = lax.broadcasted_iota(jnp.int32, (rows, scens), 0)
    zone = zone_ref[0].astype(F32)
    share_ref[...] = sums + jnp.where(scen_row == total + me, zone, 0.0)


def prices(shares, zones, total, regions, zone):
    ids = lax.broadcasted_iota(jnp.int32, shares.shape, 0)
    in_region = lax.rem(ids, regions) == lax.axis_index("region")
    gain = jnp.where(in_region & (zones == zone), ZONE_GAIN, 0.0) + SYSTEM_GAIN
    return jnp.sum(gain * shares, axis=0, keepdims=True)


def second_kernel(
    total, regions, buffer_of, zone_ref, lin_ref, v_ref, kh_ref, kl_ref, cap_ref, own_ref, shares_ref, *refs
):
    buffers = max(buffer_of) + 1
    got = refs[:buffers]
    edge_ref, rest_ref, lin2_ref = refs[buffers:]
    scens = lin_ref.shape[0]
    slots = len(buffer_of)
    lines = own_ref.shape[1] // slots
    pieces = lines // LANES
    bus_id = lax.broadcasted_iota(jnp.int32, (BOUNDARY, LANES), 0).astype(F32)
    counts = [None] * buffers
    for p in range(slots):
        b = buffer_of[p]
        for j in range(pieces):
            row = got[b][pl.ds(scens + SLOTS[p][2] * pieces + j, 1), :]
            there = jnp.where(bus_id == row, 1.0, 0.0).astype(BF16)
            met = dot_nt(own_ref[:, pl.ds(p * lines + j * LANES, LANES)], there)
            counts[b] = met if counts[b] is None else counts[b] + met
    counts_high, counts_low = halves(jnp.concatenate(counts, axis=1))
    high, low = halves(jnp.concatenate([g[pl.ds(0, scens), :] for g in got], axis=1))
    coupling = dot_nt(high, counts_high) + dot_nt(low, counts_high) + dot_nt(high, counts_low)
    shares = shares_ref[pl.ds(0, total), :]
    zones = shares_ref[pl.ds(total, total), :]
    price = prices(shares, zones, total, regions, zone_ref[0].astype(F32))
    price = jnp.broadcast_to(price, (8, scens)).T[:, 0:1]
    lin2_ref[:, pl.ds(0, BOUNDARY)] = lin_ref[:, pl.ds(0, BOUNDARY)] - price - coupling
    lin2_ref[:, pl.ds(BOUNDARY, BOUNDARY)] = lin_ref[:, pl.ds(BOUNDARY, BOUNDARY)] - price
    chains = scens // CHAIN_ROWS
    states = [v_ref[pl.ds(i * CHAIN_ROWS, CHAIN_ROWS), :] for i in range(chains)]
    injections, _ = run_sweeps(states, lin2_ref, cap_ref[...], kh_ref, kl_ref, INNER)
    for i, x in enumerate(injections):
        rows = pl.ds(i * CHAIN_ROWS, CHAIN_ROWS)
        edge_ref[rows, :] = x[:, :BOUNDARY]
        rest_ref[rows, :] = x[:, BOUNDARY:]


def again_kernel(weight_ref, edge_ref, rest_ref, share_ref, injection_ref):
    share_ref[...] = weighted_sums(weight_ref[...], edge_ref[...], rest_ref[...])
    injection_ref[0, pl.ds(0, BOUNDARY), :] = edge_ref[...].T
    injection_ref[0, pl.ds(BOUNDARY, BOUNDARY), :] = rest_ref[...].T


def table_kernel(buffer_of, scens, active_ref, count_ref, own_ref, *refs):
    got = refs[:-1]
    table_ref = refs[-1]
    slots, lines = table_ref.shape[:2]
    pieces = lines // LANES
    extra = own_ref.shape[0] - scens
    mine = own_ref[pl.ds(scens, extra), :].T
    theirs = [g[pl.ds(scens, extra), :].T for g in got]
    bus_id = lax.broadcasted_iota(jnp.int32, (LANES, BOUNDARY), 1).astype(F32)
    line_id = lax.broadcasted_iota(jnp.int32, (LANES, BOUNDARY), 0)
    for p in range(slots):
        number = live_lines(active_ref, count_ref, p)
        other = theirs[buffer_of[p]]
        half = 0.5 * SIGNS[p]
        for j in range(pieces):
            live = jnp.where(line_id + j * LANES < number, half, 0.0)
            at = p * pieces + j
            back = SLOTS[p][2] * pieces + j
            left = jnp.where(bus_id == mine[:, at : at + 1], live, 0.0)
            right = jnp.where(bus_id == other[:, back : back + 1], -live, 0.0)
            rows = pl.ds(j * LANES, LANES)
            table_ref[p, rows, pl.ds(0, BOUNDARY)] = left.astype(BF16)
            table_ref[p, rows, pl.ds(BOUNDARY, BOUNDARY)] = right.astype(BF16)


def final_kernel(total, regions, buffer_of, table_ref, shares1_ref, shares2_ref, own_ref, *refs):
    buffers = max(buffer_of) + 1
    got = refs[:buffers]
    flow_ref, price_ref, high_ref, low_ref = refs[buffers:]
    slot = pl.program_id(0)

    @pl.when(slot == 0)
    def _():
        for b in range(buffers):
            both = jnp.concatenate([own_ref[...], got[b][...]], axis=1)
            high, low = halves(both)
            high_ref[b] = high
            low_ref[b] = low
        shares = shares1_ref[pl.ds(0, total), :] + shares2_ref[pl.ds(0, total), :]
        zones = shares1_ref[pl.ds(total, total), :]
        for z in range(ZONES):
            price_ref[pl.ds(z, 1), :] = prices(shares, zones, total, regions, float(z))

    for p in range(len(buffer_of)):

        @pl.when(slot == p)
        def _(p=p):
            b = buffer_of[p]
            flow_ref[0, 0] = dot_nt(table_ref[0], high_ref[b]) + dot_nt(table_ref[0], low_ref[b])


def moved(x, axis, by):
    length = lax.axis_size(axis)
    return lax.ppermute(x, axis, [(i, (i + by) % length) for i in range(length)])


def body(kkt_inverse, scen_load, capacity, pair_active, tie_counts, line_index, area_zone):
    areas = lax.axis_size("area")
    regions = lax.axis_size("region")
    total = areas * regions
    _, buses, scens = scen_load.shape
    _, slots, lines = line_index.shape
    rest = buses - BOUNDARY
    index_rows = -(-slots * (lines // LANES) // 8) * 8
    share_rows = -(-2 * total // 16) * 16

    sources = []
    buffer_of = []
    for axis, move, _ in SLOTS:
        source = (axis, move % lax.axis_size(axis))
        if source not in sources:
            sources.append(source)
        buffer_of.append(sources.index(source))
    buffer_of = tuple(buffer_of)

    def f32(*shape):
        return jax.ShapeDtypeStruct(shape, F32)

    def bf16(*shape):
        return jax.ShapeDtypeStruct(shape, BF16)

    def exchange(x):
        return [moved(x, axis, -move) for axis, move in sources]

    def reduce_shares(shares):
        if (areas, regions) != (4, 2):
            return lax.psum(shares, ("area", "region"))
        shares = shares + moved(shares, "region", 1)
        return (shares + moved(shares, "area", 2)) + (moved(shares, "area", 1) + moved(shares, "area", -1))

    edge1, rest1, state, lin, kh, kl = pl.pallas_call(
        first_kernel,
        out_shape=(
            f32(scens + index_rows, BOUNDARY),
            f32(scens, rest),
            f32(scens, buses),
            f32(scens, buses),
            bf16(buses, buses),
            bf16(buses, buses),
        ),
        in_specs=[VMEM] * 4,
        out_specs=[VMEM] * 6,
        compiler_params=PARAMS,
        name="first_round",
    )(kkt_inverse, scen_load, capacity, line_index)
    got1 = exchange(edge1)
    share1, own, weights = pl.pallas_call(
        functools.partial(share_kernel, areas, regions),
        out_shape=(f32(share_rows, scens), bf16(BOUNDARY, slots * lines), f32(share_rows, buses)),
        in_specs=[SMEM] * 3 + [VMEM] * 3,
        out_specs=[VMEM] * 3,
        compiler_params=PARAMS,
        name="mismatch_shares",
    )(pair_active, tie_counts, area_zone, edge1, rest1, line_index)
    shares1 = reduce_shares(share1)
    edge2, rest2 = pl.pallas_call(
        functools.partial(second_kernel, total, regions, buffer_of),
        out_shape=(f32(scens, BOUNDARY), f32(scens, rest)),
        in_specs=[SMEM] + [VMEM] * (7 + len(got1)),
        out_specs=[VMEM] * 2,
        scratch_shapes=[pltpu.VMEM((scens, buses), F32)],
        compiler_params=PARAMS,
        name="second_round",
    )(area_zone, lin, state, kh, kl, capacity, own, shares1, *got1)
    got2 = exchange(edge2)
    share2, injection = pl.pallas_call(
        again_kernel,
        out_shape=(f32(share_rows, scens), f32(1, buses, scens)),
        in_specs=[VMEM] * 3,
        out_specs=[VMEM] * 2,
        compiler_params=PARAMS,
        name="mismatch_shares_again",
    )(weights, edge2, rest2)
    shares2 = reduce_shares(share2)
    table = pl.pallas_call(
        functools.partial(table_kernel, buffer_of, scens),
        out_shape=bf16(slots, lines, 2 * BOUNDARY),
        in_specs=[SMEM] * 2 + [VMEM] * (1 + len(got1)),
        out_specs=VMEM,
        compiler_params=PARAMS,
        name="line_table",
    )(pair_active, tie_counts, edge1, *got1)
    flow, price = pl.pallas_call(
        functools.partial(final_kernel, total, regions, buffer_of),
        out_shape=(f32(1, slots, lines, scens), f32(ZONES, scens)),
        grid=(slots,),
        in_specs=[pl.BlockSpec((1, lines, 2 * BOUNDARY), lambda p: (p, 0, 0))]
        + [pl.BlockSpec((share_rows, scens), lambda p: (0, 0))] * 2
        + [pl.BlockSpec((scens, BOUNDARY), lambda p: (0, 0))] * (1 + len(got2)),
        out_specs=(
            pl.BlockSpec((1, 1, lines, scens), lambda p: (0, p, 0, 0)),
            pl.BlockSpec((ZONES, scens), lambda p: (0, 0)),
        ),
        scratch_shapes=[pltpu.VMEM((len(got2), scens, 2 * BOUNDARY), BF16)] * 2,
        compiler_params=PARAMS,
        name="tie_flows",
    )(table, shares1, shares2, edge2, *got2)
    return injection, flow, price


def solution(mesh):
    placed = (
        P(("area", "region"), None, None),
        P(("area", "region"), None, ("group", "scen")),
        P(("area", "region"), None),
        P(("area", "region"), None),
        P(("area", "region"), None),
        P(("area", "region"), None, None),
        P(("area", "region")),
    )
    return jax.shard_map(
        body,
        mesh=mesh,
        in_specs=placed,
        out_specs=(
            P(("area", "region"), None, ("group", "scen")),
            P(("area", "region"), None, None, ("group", "scen")),
            P("region", ("group", "scen")),
        ),
        check_vma=False,
    )
```

```python
import functools

import jax
import jax.numpy as jnp
from jax import lax
from jax.experimental import pallas as pl
from jax.experimental.pallas import tpu as pltpu
from jax.sharding import PartitionSpec as P

ZONES = 4
INNER = 24
BOUNDARY = 128
LANES = 128
ZONE_GAIN = 0.004
SYSTEM_GAIN = 0.001
SLOTS = (
    ("area", 1, 1),
    ("area", -1, 0),
    ("area", 2, 3),
    ("area", -2, 2),
    ("region", 1, 5),
    ("region", -1, 4),
)
SIGNS = (1.0, -1.0, 1.0, -1.0, 1.0, -1.0)
CHAIN_ROWS = 32
UNROLL = 4
BIG = 10**11
SMALL = 10**9

F32 = jnp.float32
BF16 = jnp.bfloat16
VMEM = pl.BlockSpec(memory_space=pltpu.VMEM)
HBM = pl.BlockSpec(memory_space=pltpu.HBM)
FIRST_VMEM = 56 * 2**20
PARAMS = pltpu.CompilerParams(vmem_limit_bytes=40 * 2**20)


def dot(a, b):
    return jnp.dot(a, b, preferred_element_type=F32)


def dot_nt(a, b):
    return lax.dot_general(a, b, (((1,), (1,)), ((), ())), preferred_element_type=F32)


def halves(x):
    high = x.astype(BF16)
    return high, (x - high.astype(F32)).astype(BF16)


def thirds(x):
    high = x.astype(BF16)
    rest = x - high.astype(F32)
    middle = rest.astype(BF16)
    return high, middle, (rest - middle.astype(F32)).astype(BF16)


def clipping(v, limits):
    clipped = jnp.clip(v, -limits, limits)
    return clipped, v - clipped


def run_sweeps(start, finish, lin_ref, over_ref, limits, kh_ref, kl_ref, count):
    scens, buses = lin_ref.shape
    chains = scens // CHAIN_ROWS

    def scoped(*accumulators):
        highs, lows = accumulators[:chains], accumulators[chains:]
        pltpu.matmul_push_rhs(kh_ref[...], 0, 0)
        pltpu.matmul_push_rhs(kl_ref[...], 0, 1)

        def issue(i, x, load=None):
            high, low = halves(x)
            pltpu.matmul_acc_lhs(highs[i], high, load)
            pltpu.matmul_acc_lhs(highs[i], low)
            pltpu.matmul_acc_lhs(lows[i], high, load)

        def rows_of(i):
            return pl.ds(i * CHAIN_ROWS, CHAIN_ROWS)

        def taken(i):
            return pltpu.matmul_pop(highs[i]) + pltpu.matmul_pop(lows[i])

        for i in range(chains):
            x, over = start(rows_of(i))
            over_ref[rows_of(i), :] = over
            issue(i, x, 0 if i == 0 else None)

        def sweep(_, carry):
            for i in range(chains):
                rows = rows_of(i)
                clipped, over = clipping(taken(i) + over_ref[rows, :], limits)
                over_ref[rows, :] = over
                issue(i, lin_ref[rows, :] + (clipped - over))
            return carry

        lax.fori_loop(0, count - 1, sweep, 0, unroll=UNROLL)
        for i in range(chains):
            finish(rows_of(i), taken(i), over_ref[rows_of(i), :])

    pl.run_scoped(
        scoped,
        *[pltpu.ACC(0)((CHAIN_ROWS, buses), F32)] * chains,
        *[pltpu.ACC(1)((CHAIN_ROWS, buses), F32)] * chains,
    )


def line_tables(areas, regions, slots, pieces, near, idx_row, number, own_ref, rows):
    me_area, me_region = lax.axis_index("area"), lax.axis_index("region")
    here = me_area if near else me_area * regions + me_region
    width = -(-rows // LANES) * LANES
    row_id = lax.broadcasted_iota(jnp.int32, (1, width), 1)
    line_id = lax.broadcasted_iota(jnp.int32, (1, LANES), 1).astype(F32)
    bus_id = lax.broadcasted_iota(jnp.int32, (BOUNDARY, LANES), 0).astype(F32)
    weights = jnp.zeros((BOUNDARY, width), F32)
    for p in range(slots):
        axis, move, _ = SLOTS[p]
        if axis == "area":
            other = lax.rem(me_area + move % areas, areas)
            there = other if near else other * regions + me_region
        else:
            there = areas + 1 if near else me_area * regions + lax.rem(me_region + move % regions, regions)
        coefficient = jnp.where(row_id == there, 0.5, 0.0) - jnp.where(row_id == here, 0.5, 0.0)
        met = None
        for j in range(pieces):
            row = jnp.where(line_id + float(j * LANES) < number(p), idx_row(p, j), -1.0)
            onehot = jnp.where(bus_id == row, 1.0, 0.0)
            own_ref[:, pl.ds((p * pieces + j) * LANES, LANES)] = onehot.astype(BF16)
            met = onehot if met is None else met + onehot
        weights = weights + jnp.sum(met, axis=1, keepdims=True) * coefficient
    last = areas if near else areas * regions
    mine = jnp.where((row_id == here) | (row_id == last), 1.0, 0.0)
    weights = jnp.concatenate([weights + mine, jnp.broadcast_to(mine, (BOUNDARY, width))], axis=0)
    return weights.T[0:rows, :]


def weighted_sums(weights, x):
    wh, wl = halves(weights)
    xh, xm, xl = thirds(x)
    return dot_nt(wh, xh) + (dot_nt(wh, xm) + dot_nt(wl, xh)) + (dot_nt(wh, xl) + dot_nt(wl, xm))


def store_shares(areas, near, sums, share_refs):
    share_refs[0][...] = sums[0 : share_refs[0].shape[0], :]
    if near:
        row_id = lax.broadcasted_iota(jnp.int32, (8, sums.shape[1]), 0)
        across = jnp.where(row_id == lax.axis_index("area"), sums[areas + 1 : areas + 2, :], 0.0)
        share_refs[1][...] = jnp.where(row_id == areas, sums[areas : areas + 1, :], across)


def first_kernel(
    areas, regions, near, base,
    k_hbm, load_hbm, cap_hbm, idx_hbm, active_hbm, count_hbm, zone_hbm,
    edge_ref, rest_ref, v_ref, lin_hbm, kh_hbm, kl_hbm, own_hbm, cap_out_ref, weight_ref,
    k_ref, load_ref, cap_ref, idx_ref, active_ref, count_ref, zone_ref,
    lin_ref, kh_ref, kl_ref, own_ref, over_ref, sems, out_sems,
):
    pairs = (
        (k_hbm, k_ref),
        (load_hbm, load_ref),
        (cap_hbm, cap_ref),
        (idx_hbm, idx_ref),
        (active_hbm, active_ref),
        (count_hbm, count_ref),
        (zone_hbm, zone_ref),
    )
    copies = [pltpu.make_async_copy(src, dst, sems.at[i]) for i, (src, dst) in enumerate(pairs)]
    for copy in copies:
        copy.start()
    pairs = ((kh_ref, kh_hbm), (kl_ref, kl_hbm), (lin_ref, lin_hbm), (own_ref, own_hbm))
    results = [pltpu.make_async_copy(src, dst, out_sems.at[i]) for i, (src, dst) in enumerate(pairs)]
    scens = lin_ref.shape[0]
    slots, _, lines = idx_ref.shape
    pieces = lines // LANES
    for copy in copies[3:]:
        copy.wait()
    numbers = jnp.where(active_ref[...] > 0, count_ref[...], 0).astype(F32)

    def idx_row(p, j):
        return idx_ref[p, :, pl.ds(j * LANES, LANES)].astype(F32)

    edge_ref[pl.ds(base, edge_ref.shape[0] - base), :] = jnp.zeros((edge_ref.shape[0] - base, LANES), F32)
    for p in range(slots):
        for j in range(pieces):
            edge_ref[pl.ds(base + p * pieces + j, 1), :] = idx_row(p, j)
    edge_ref[pl.ds(base + slots * pieces, 1), pl.ds(0, slots)] = numbers
    zone = zone_ref[0].astype(F32)
    edge_ref[pl.ds(base + slots * pieces + 1, 1), :] = jnp.full((1, LANES), zone)
    weight_ref[...] = line_tables(
        areas, regions, slots, pieces, near, idx_row, lambda p: numbers[:, p : p + 1], own_ref, weight_ref.shape[0]
    )
    copies[0].wait()
    high, low = halves(k_ref[0].T)
    kh_ref[...] = high
    kl_ref[...] = low
    copies[1].wait()
    lin_ref[...] = load_ref[0].T
    copies[2].wait()
    cap_out_ref[...] = cap_ref[...]
    for copy in results:
        copy.start()
    limits = cap_ref[...]

    def start(rows):
        return lin_ref[rows, :], jnp.zeros((CHAIN_ROWS, lin_ref.shape[1]), F32)

    def finish(rows, x, over):
        edge_ref[rows, :] = x[:, :BOUNDARY]
        rest_ref[rows, :] = x[:, BOUNDARY:]
        v_ref[rows, :] = x + over

    run_sweeps(start, finish, lin_ref, over_ref, limits, kh_ref, kl_ref, INNER)
    for copy in results:
        copy.wait()


def share_kernel(areas, regions, near, zone_at, weight_ref, edge_ref, rest_ref, *share_refs):
    scens = rest_ref.shape[0]
    x = jnp.concatenate([edge_ref[pl.ds(0, scens), :], rest_ref[...]], axis=1)
    sums = weighted_sums(weight_ref[...], x)
    if zone_at is not None:
        me = lax.axis_index("area") * regions + lax.axis_index("region")
        zone = edge_ref[pl.ds(zone_at, 1), pl.ds(0, 1)]
        row_id = lax.broadcasted_iota(jnp.int32, sums.shape, 0)
        sums = sums + jnp.where(row_id == areas * regions + 1 + me, zone, 0.0)
    store_shares(areas, near, sums, share_refs)


def live_lines(edge_ref, base, slots, pieces, p):
    return edge_ref[pl.ds(base + slots * pieces, 1), pl.ds(p, 1)]


def by_area(values):
    me = lax.axis_index("area")
    out = []
    for k in range(4):
        mask = jnp.bitwise_xor(me, k)
        low = jnp.where(jnp.bitwise_and(mask, 1) == 0, values[0], values[1])
        high = jnp.where(jnp.bitwise_and(mask, 1) == 0, values[2], values[3])
        out.append(jnp.where(mask < 2, low, high))
    return out


def near_zones(at, own_ref, got):
    return by_area([ref[pl.ds(at, 1), pl.ds(0, 1)] for ref in (own_ref, got[2], got[1], got[0])])


def near_prices(sums, zones, zone):
    price = sums[4:5, :] * SYSTEM_GAIN
    for k in range(4):
        price = price + jnp.where(zones[k] == zone, ZONE_GAIN, 0.0) * sums[k : k + 1, :]
    return price


def prices(shares, zones, total, regions, zone):
    ids = lax.broadcasted_iota(jnp.int32, zones.shape, 0)
    in_region = lax.rem(ids, regions) == lax.axis_index("region")
    gain = jnp.where(in_region & (zones == zone), ZONE_GAIN, 0.0) + SYSTEM_GAIN
    return jnp.sum(gain * shares[0:total, :], axis=0, keepdims=True)


class Mask(int):
    pass


def by_slot(buffer_of, got):
    even = lax.rem(lax.axis_index("area"), 2) == 0

    def read(p, rows):
        choice = buffer_of[p]
        if isinstance(choice, int):
            return got[choice][rows, :]
        return jnp.where(even, got[choice[0]][rows, :], got[choice[1]][rows, :])

    return read


def coupling_kernel(slots_of, scens, base, pieces, own_ref, *refs):
    got = refs[: len(slots_of)]
    coupling_ref = refs[-1]
    before = refs[len(slots_of) : -1]
    even = lax.rem(lax.axis_index("area"), 2) == 0
    lines = pieces * LANES
    bus_id = lax.broadcasted_iota(jnp.int32, (BOUNDARY, LANES), 0).astype(F32)
    counts = []
    for g, served in zip(got, slots_of):
        met = jnp.zeros((BOUNDARY, BOUNDARY), F32)
        for pair in served:
            for j in range(pieces):
                if isinstance(pair, int):
                    mine = own_ref[:, pl.ds(pair * lines + j * LANES, LANES)]
                    row = g[pl.ds(base + SLOTS[pair][2] * pieces + j, 1), :]
                else:
                    mine, row = [], []
                    for p in pair:
                        mine.append(own_ref[:, pl.ds(p * lines + j * LANES, LANES)])
                        row.append(g[pl.ds(base + SLOTS[p][2] * pieces + j, 1), :])
                    mine = jnp.where(even, *mine)
                    row = jnp.where(even, *row)
                there = jnp.where(bus_id == row, 1.0, 0.0).astype(BF16)
                met = met + dot_nt(mine, there)
        counts.append(met)
    counts_high, counts_low = halves(jnp.concatenate(counts, axis=1))
    high, low = halves(jnp.concatenate([g[pl.ds(0, scens), :] for g in got], axis=1))
    out = dot_nt(high, counts_high) + dot_nt(low, counts_high) + dot_nt(high, counts_low)
    for ref in before:
        out = out + ref[...]
    coupling_ref[...] = out


def second_kernel(
    areas, regions, near, info, lin_ref, coupling_ref, v_ref, kh_ref, kl_ref, cap_ref, edge1_ref, *refs
):
    edge_ref, rest_ref, sums_ref, lin2_ref, over_ref = refs[-5:]
    refs = refs[:-5]
    scens = lin_ref.shape[0]
    zone = edge1_ref[pl.ds(info + 1, 1), pl.ds(0, 1)]
    if near:
        sums = refs[0][...] + refs[1][...]
        zones = near_zones(info + 1, edge1_ref, refs[2:])
        price = near_prices(sums, zones, zone)
        sums_ref[pl.ds(0, 8), :] = sums
        sums_ref[pl.ds(8, 8), :] = jnp.zeros((8, scens), F32)
        for k in range(4):
            sums_ref[pl.ds(8 + k, 1), :] = jnp.broadcast_to(zones[k], (1, scens))
    else:
        total = areas * regions
        sums = refs[0][...]
        sums_ref[...] = sums
        price = prices(sums, sums[total + 1 : 2 * total + 1, :], total, regions, zone)
    price = jnp.broadcast_to(price, (8, scens)).T[:, 0:1]
    lin2_ref[:, pl.ds(0, BOUNDARY)] = lin_ref[:, pl.ds(0, BOUNDARY)] - price - coupling_ref[...]
    lin2_ref[:, pl.ds(BOUNDARY, BOUNDARY)] = lin_ref[:, pl.ds(BOUNDARY, BOUNDARY)] - price
    limits = cap_ref[...]

    def start(rows):
        clipped, over = clipping(v_ref[rows, :], limits)
        return lin2_ref[rows, :] + (clipped - over), over

    def finish(rows, x, over):
        edge_ref[rows, :] = x[:, :BOUNDARY]
        rest_ref[rows, :] = x[:, BOUNDARY:]

    run_sweeps(start, finish, lin2_ref, over_ref, limits, kh_ref, kl_ref, INNER)


def injection_kernel(edge_ref, rest_ref, injection_ref):
    scens = rest_ref.shape[0]
    injection_ref[0, pl.ds(0, BOUNDARY), :] = edge_ref[pl.ds(0, scens), :].T
    injection_ref[0, pl.ds(BOUNDARY, BOUNDARY), :] = rest_ref[...].T


def table_kernel(buffer_of, base, own_ref, *refs):
    got = refs[:-2]
    mine_ref, theirs_ref = refs[-2:]
    slots, lines = mine_ref.shape[:2]
    pieces = lines // LANES
    extra = own_ref.shape[0] - base
    read = by_slot(buffer_of, got)
    mine = own_ref[pl.ds(base, extra), :].T
    bus_id = lax.broadcasted_iota(jnp.int32, (LANES, BOUNDARY), 1).astype(F32)
    line_id = lax.broadcasted_iota(jnp.int32, (LANES, BOUNDARY), 0).astype(F32)
    for p in range(slots):
        number = live_lines(own_ref, base, slots, pieces, p)
        other = read(p, pl.ds(base, extra)).T
        half = 0.5 * SIGNS[p]
        for j in range(pieces):
            live = jnp.where(line_id + float(j * LANES) < number, half, 0.0)
            at = p * pieces + j
            back = SLOTS[p][2] * pieces + j
            rows = pl.ds(j * LANES, LANES)
            mine_ref[p, rows, :] = jnp.where(bus_id == mine[:, at : at + 1], live, 0.0).astype(BF16)
            theirs_ref[p, rows, :] = jnp.where(bus_id == other[:, back : back + 1], -live, 0.0).astype(BF16)


def twice(x):
    return jnp.concatenate([x, x], axis=1)


def own_kernel(table_ref, edge_ref, flow_ref):
    scens = flow_ref.shape[2]
    parts = jnp.concatenate(halves(edge_ref[pl.ds(0, scens), :]), axis=1)
    for p in range(table_ref.shape[0]):
        flow_ref[p] = dot_nt(twice(table_ref[p]), parts)


def parts_kernel(*refs):
    buffers = len(refs) // 2
    for b in range(buffers):
        refs[buffers + b][...] = jnp.concatenate(halves(refs[b][...]), axis=1)


def final_kernel(areas, regions, near, buffer_of, buffers, ready, table_ref, own_ref, sums_ref, *refs):
    flow_hbm, price_ref, flow_ref, late_ref, sems = refs[-5:]
    parts = list(refs[:ready])
    for i, ref in enumerate(refs[ready:buffers]):
        late_ref[i] = jnp.concatenate(halves(ref[...]), axis=1)
        parts.append(late_ref.at[i])
    read = by_slot(buffer_of, parts)
    scens = flow_ref.shape[2]
    copies = []
    for p in range(len(buffer_of)):
        flow_ref[p] = own_ref[p] + dot_nt(twice(table_ref[p]), read(p, pl.ds(0, scens)))
        copies.append(pltpu.make_async_copy(flow_ref.at[p], flow_hbm.at[0, p], sems.at[p]))
        copies[-1].start()
    rest = refs[buffers:-5]
    if near:
        sums = sums_ref[pl.ds(0, 8), :] + (rest[0][...] + rest[1][...])
        zones = [sums_ref[pl.ds(8 + k, 1), :] for k in range(4)]
        for z in range(ZONES):
            price_ref[pl.ds(z, 1), :] = near_prices(sums, zones, float(z))
    else:
        total = areas * regions
        first = sums_ref[...]
        zones = first[total + 1 : 2 * total + 1, :]
        for z in range(ZONES):
            price_ref[pl.ds(z, 1), :] = prices(first + rest[0][...], zones, total, regions, float(z))
    for copy in copies:
        copy.wait()


def moved(x, axis, by):
    length = lax.axis_size(axis)
    if isinstance(by, Mask):
        return lax.ppermute(x, axis, [(i, i ^ by) for i in range(length)])
    return lax.ppermute(x, axis, [((i + by) % length, i) for i in range(length)])


def body(kkt_inverse, scen_load, capacity, pair_active, tie_counts, line_index, area_zone):
    areas = lax.axis_size("area")
    regions = lax.axis_size("region")
    total = areas * regions
    _, buses, scens = scen_load.shape
    _, slots, lines = line_index.shape
    rest = buses - BOUNDARY
    pieces = lines // LANES
    near = (areas, regions) == (4, 2)
    base = scens
    info = base + slots * pieces
    edge1_rows = -(-(info + 2) // 8) * 8
    share_rows = 8 if near else -(-(2 * total + 1) // 8) * 8
    weight_rows = -(-share_rows // 16) * 16

    if areas == 4:
        sources = [("area", Mask(3)), ("area", Mask(2)), ("area", Mask(1))]
        buffer_of = [(2, 0), (0, 2), 1, 1]
        slots_of = [((1, 0),), (2, 3), ((0, 1),)]
        ready = 2
    else:
        sources = [("area", move) for _, move, _ in SLOTS[:4]]
        buffer_of = [0, 1, 2, 3]
        slots_of = [(0,), (1,), (2,), (3,)]
        ready = 4
    for p, (axis, move, _) in enumerate(SLOTS[4:], 4):
        source = (axis, move % regions)
        if source not in sources:
            sources.append(source)
            slots_of.append(())
        buffer_of.append(sources.index(source))
        slots_of[-1] += (p,)
    buffer_of = tuple(buffer_of)

    def f32(*shape):
        return jax.ShapeDtypeStruct(shape, F32)

    def bf16(*shape):
        return jax.ShapeDtypeStruct(shape, BF16)

    def exchange(x):
        return [moved(x, axis, move) for axis, move in sources[::-1]][::-1]

    def reduce_shares(shares):
        if not near:
            return [lax.psum(shares[0], ("area", "region"))]
        sums = shares[0] + moved(shares[1], "region", 1)
        sums = sums + moved(sums, "area", Mask(1))
        return [sums, moved(sums, "area", Mask(2))]

    def cost(flops):
        return pl.CostEstimate(flops=flops, bytes_accessed=0, transcendentals=0)

    edge1, rest1, state, lin, kh, kl, own, limits, weights = pl.pallas_call(
        functools.partial(first_kernel, areas, regions, near, base),
        out_shape=[
            f32(edge1_rows, BOUNDARY),
            f32(scens, rest),
            f32(scens, buses),
            f32(scens, buses),
            bf16(buses, buses),
            bf16(buses, buses),
            bf16(BOUNDARY, slots * lines),
            f32(1, buses),
            f32(weight_rows, buses),
        ],
        in_specs=[HBM] * 7,
        out_specs=[VMEM] * 3 + [HBM] * 4 + [VMEM] * 2,
        scratch_shapes=[
            pltpu.VMEM((1, buses, buses), F32),
            pltpu.VMEM((1, buses, scens), F32),
            pltpu.VMEM((1, buses), F32),
            pltpu.VMEM((slots, 1, lines), jnp.int32),
            pltpu.VMEM((1, slots), jnp.int32),
            pltpu.VMEM((1, slots), jnp.int32),
            pltpu.SMEM((1,), jnp.int32),
            pltpu.VMEM((scens, buses), F32),
            pltpu.VMEM((buses, buses), BF16),
            pltpu.VMEM((buses, buses), BF16),
            pltpu.VMEM((BOUNDARY, slots * lines), BF16),
            pltpu.VMEM((scens, buses), F32),
            pltpu.SemaphoreType.DMA((7,)),
            pltpu.SemaphoreType.DMA((4,)),
        ],
        compiler_params=pltpu.CompilerParams(vmem_limit_bytes=FIRST_VMEM),
        name="first_round",
    )(kkt_inverse, scen_load, capacity, line_index.reshape(slots, 1, lines), pair_active, tie_counts, area_zone)

    def make_shares(edge, rest, zone_at):
        return pl.pallas_call(
            functools.partial(share_kernel, areas, regions, near, zone_at),
            out_shape=[f32(share_rows, scens)] * (2 if near else 1),
            in_specs=[VMEM] * 3,
            out_specs=[VMEM] * (2 if near else 1),
            compiler_params=PARAMS,
            name="mismatch_shares",
        )(weights, edge, rest)

    sums1 = reduce_shares(make_shares(edge1, rest1, None if near else info + 1))
    got1 = exchange(edge1)
    coupling = ()
    for which, estimate in ((slice(0, ready), BIG), (slice(ready, None), SMALL)):
        coupling = pl.pallas_call(
            functools.partial(coupling_kernel, slots_of[which], scens, base, pieces),
            out_shape=(f32(scens, BOUNDARY),),
            in_specs=[VMEM] * (1 + len(got1[which]) + len(coupling)),
            out_specs=(VMEM,),
            compiler_params=PARAMS,
            cost_estimate=cost(estimate),
            name="coupling",
        )(own, *got1[which], *coupling)
    sources1 = [*sums1, *got1] if near else sums1
    edge2, rest2, first = pl.pallas_call(
        functools.partial(second_kernel, areas, regions, near, info),
        out_shape=[
            f32(scens, BOUNDARY),
            f32(scens, rest),
            f32(16 if near else share_rows, scens),
        ],
        in_specs=[VMEM] * (7 + len(sources1)),
        out_specs=[VMEM] * 3,
        scratch_shapes=[pltpu.VMEM((scens, buses), F32)] * 2,
        compiler_params=PARAMS,
        name="second_round",
    )(lin, *coupling, state, kh, kl, limits, edge1, *sources1)
    sums2 = reduce_shares(make_shares(edge2, rest2, None))
    got2 = exchange(edge2)
    injection = pl.pallas_call(
        injection_kernel,
        out_shape=f32(1, buses, scens),
        in_specs=[VMEM] * 2,
        out_specs=VMEM,
        compiler_params=PARAMS,
        name="injection",
    )(edge2, rest2)
    mine, theirs = pl.pallas_call(
        functools.partial(table_kernel, buffer_of, base),
        out_shape=(bf16(slots, lines, BOUNDARY),) * 2,
        in_specs=[VMEM] * (1 + len(got1)),
        out_specs=[VMEM] * 2,
        compiler_params=PARAMS,
        name="line_table",
    )(edge1, *got1)
    own_flow = pl.pallas_call(
        own_kernel,
        out_shape=f32(slots, lines, scens),
        in_specs=[VMEM] * 2,
        out_specs=VMEM,
        compiler_params=PARAMS,
        name="own_flows",
    )(mine, edge2)
    parts = pl.pallas_call(
        parts_kernel,
        out_shape=[bf16(scens, 2 * BOUNDARY)] * ready,
        in_specs=[VMEM] * ready,
        out_specs=[VMEM] * ready,
        compiler_params=PARAMS,
        cost_estimate=cost(BIG),
        name="injection_parts",
    )(*got2[:ready])
    flow, price = pl.pallas_call(
        functools.partial(final_kernel, areas, regions, near, buffer_of, len(got2), ready),
        out_shape=(f32(1, slots, lines, scens), f32(ZONES, scens)),
        in_specs=[VMEM] * (3 + len(got2) + len(sums2)),
        out_specs=(HBM, VMEM),
        scratch_shapes=[
            pltpu.VMEM((slots, lines, scens), F32),
            pltpu.VMEM((len(got2) - ready, scens, 2 * BOUNDARY), BF16),
            pltpu.SemaphoreType.DMA((slots,)),
        ],
        compiler_params=PARAMS,
        name="tie_flows",
    )(theirs, own_flow, first, *parts, *got2[ready:], *sums2)
    return injection, flow, price


def solution(mesh):
    placed = (
        P(("area", "region"), None, None),
        P(("area", "region"), None, ("group", "scen")),
        P(("area", "region"), None),
        P(("area", "region"), None),
        P(("area", "region"), None),
        P(("area", "region"), None, None),
        P(("area", "region")),
    )
    return jax.shard_map(
        body,
        mesh=mesh,
        in_specs=placed,
        out_specs=(
            P(("area", "region"), None, ("group", "scen")),
            P(("area", "region"), None, None, ("group", "scen")),
            P("region", ("group", "scen")),
        ),
        check_vma=False,
    )
```

```python
import functools

import jax
import jax.numpy as jnp
from jax import lax
from jax.experimental import pallas as pl
from jax.experimental.pallas import tpu as pltpu
from jax.sharding import PartitionSpec as P

ZONES = 4
INNER = 24
BOUNDARY = 128
LANES = 128
ZONE_GAIN = 0.004
SYSTEM_GAIN = 0.001
SLOTS = (
    ("area", 1, 1),
    ("area", -1, 0),
    ("area", 2, 3),
    ("area", -2, 2),
    ("region", 1, 5),
    ("region", -1, 4),
)
SIGNS = (1.0, -1.0, 1.0, -1.0, 1.0, -1.0)
CHAIN_ROWS = 32
UNROLL = 4
BIG = 4 * 10**9
OPENING = 10**11

F32 = jnp.float32
BF16 = jnp.bfloat16
VMEM = pl.BlockSpec(memory_space=pltpu.VMEM)
SMEM = pl.BlockSpec(memory_space=pltpu.SMEM)
HBM = pl.BlockSpec(memory_space=pltpu.HBM)
PARAMS = pltpu.CompilerParams(vmem_limit_bytes=40 * 2**20)


def dot(a, b):
    return jnp.dot(a, b, preferred_element_type=F32)


def dot_nt(a, b):
    return lax.dot_general(a, b, (((1,), (1,)), ((), ())), preferred_element_type=F32)


def halves(x):
    high = x.astype(BF16)
    return high, (x - high.astype(F32)).astype(BF16)


def thirds(x):
    high = x.astype(BF16)
    rest = x - high.astype(F32)
    middle = rest.astype(BF16)
    return high, middle, (rest - middle.astype(F32)).astype(BF16)


def clipping(v, limits):
    clipped = jnp.clip(v, -limits, limits)
    return clipped, v - clipped


def run_sweeps(start, finish, lin_ref, over_ref, limits, kh_ref, kl_ref, count):
    scens, buses = lin_ref.shape
    chains = scens // CHAIN_ROWS

    def scoped(*accumulators):
        highs, lows = accumulators[:chains], accumulators[chains:]
        pltpu.matmul_push_rhs(kh_ref[...], 0, 0)
        pltpu.matmul_push_rhs(kl_ref[...], 0, 1)

        def issue(i, x, load=None):
            high, low = halves(x)
            pltpu.matmul_acc_lhs(highs[i], high, load)
            pltpu.matmul_acc_lhs(highs[i], low)
            pltpu.matmul_acc_lhs(lows[i], high, load)

        def rows_of(i):
            return pl.ds(i * CHAIN_ROWS, CHAIN_ROWS)

        def taken(i):
            return pltpu.matmul_pop(highs[i]) + pltpu.matmul_pop(lows[i])

        for i in range(chains):
            x, over = start(rows_of(i))
            over_ref[rows_of(i), :] = over
            issue(i, x, 0 if i == 0 else None)

        def sweep(_, carry):
            for i in range(chains):
                rows = rows_of(i)
                clipped, over = clipping(taken(i) + over_ref[rows, :], limits)
                over_ref[rows, :] = over
                issue(i, lin_ref[rows, :] + (clipped - over))
            return carry

        lax.fori_loop(0, count - 1, sweep, 0, unroll=UNROLL)
        for i in range(chains):
            finish(rows_of(i), taken(i), over_ref[rows_of(i), :])

    pl.run_scoped(
        scoped,
        *[pltpu.ACC(0)((CHAIN_ROWS, buses), F32)] * chains,
        *[pltpu.ACC(1)((CHAIN_ROWS, buses), F32)] * chains,
    )


def line_tables(areas, regions, slots, pieces, near, idx_row, number, own_ref, rows):
    me_area, me_region = lax.axis_index("area"), lax.axis_index("region")
    here = me_area if near else me_area * regions + me_region
    width = -(-rows // LANES) * LANES
    row_id = lax.broadcasted_iota(jnp.int32, (1, width), 1)
    line_id = lax.broadcasted_iota(jnp.int32, (1, LANES), 1).astype(F32)
    bus_id = lax.broadcasted_iota(jnp.int32, (BOUNDARY, LANES), 0).astype(F32)
    weights = jnp.zeros((BOUNDARY, width), F32)
    for p in range(slots):
        axis, move, _ = SLOTS[p]
        if axis == "area":
            other = lax.rem(me_area + move % areas, areas)
            there = other if near else other * regions + me_region
        else:
            there = areas + 1 if near else me_area * regions + lax.rem(me_region + move % regions, regions)
        coefficient = jnp.where(row_id == there, 0.5, 0.0) - jnp.where(row_id == here, 0.5, 0.0)
        met = None
        for j in range(pieces):
            row = jnp.where(line_id + float(j * LANES) < number(p), idx_row(p, j), -1.0)
            onehot = jnp.where(bus_id == row, 1.0, 0.0)
            own_ref[:, pl.ds((p * pieces + j) * LANES, LANES)] = onehot.astype(BF16)
            met = onehot if met is None else met + onehot
        weights = weights + jnp.sum(met, axis=1, keepdims=True) * coefficient
    last = areas if near else areas * regions
    mine = jnp.where((row_id == here) | (row_id == last), 1.0, 0.0)
    weights = jnp.concatenate([weights + mine, jnp.broadcast_to(mine, (BOUNDARY, width))], axis=0)
    return weights.T[0:rows, :]


def weighted_sums(weights, x):
    wh, wl = halves(weights)
    xh, xm, xl = thirds(x)
    return dot_nt(wh, xh) + (dot_nt(wh, xm) + dot_nt(wl, xh)) + (dot_nt(wh, xl) + dot_nt(wl, xm))


def folded(x):
    return jnp.concatenate([x[:, j : j + LANES] for j in range(0, x.shape[1], LANES)], axis=0)


def unfolded(x):
    return jnp.concatenate([x[j : j + 8, :] for j in range(0, x.shape[0], 8)], axis=1)


def opening_kernel(zeros_ref):
    zeros_ref[...] = jnp.zeros(zeros_ref.shape, F32)


def first_kernel(
    areas, regions, near, zeros_ref, k_ref, load_ref, cap_ref, idx_ref, active_ref, count_ref, zone_ref, *refs
):
    edge_ref, *lean_refs = refs[:-8]
    rest_ref, v_ref, lin_ref, kh_ref, kl_ref, own_ref, weight_ref, over_ref = refs[-8:]
    scens = lin_ref.shape[0]
    slots, _, lines = idx_ref.shape
    pieces = lines // LANES
    numbers = jnp.where(active_ref[...] > 0, count_ref[...], 0).astype(F32)
    zone = jnp.full((1, LANES), zone_ref[0].astype(F32))

    def idx_row(p, j):
        return idx_ref[p, :, pl.ds(j * LANES, LANES)].astype(F32)

    for ref, held in ((edge_ref, range(slots)), *zip(lean_refs, ((2, 3), (4, 5)))):
        ref[pl.ds(ref.shape[0] - 8, 8), :] = zeros_ref[...]
        at = scens
        for p in held:
            for j in range(pieces):
                ref[pl.ds(at, 1), :] = idx_row(p, j)
                at += 1
        ref[pl.ds(at, 1), :] = zone
    edge_ref[pl.ds(scens + slots * pieces + 1, 1), pl.ds(0, slots)] = numbers
    weight_ref[...] = line_tables(
        areas, regions, slots, pieces, near, idx_row, lambda p: numbers[:, p : p + 1], own_ref, weight_ref.shape[0]
    )
    high, low = halves(k_ref[0].T)
    kh_ref[...] = high
    kl_ref[...] = low
    lin_ref[...] = load_ref[0].T
    limits = cap_ref[...]

    def start(rows):
        return lin_ref[rows, :], jnp.zeros((CHAIN_ROWS, lin_ref.shape[1]), F32)

    def finish(rows, x, over):
        for ref in (edge_ref, *lean_refs):
            ref[rows, :] = x[:, :BOUNDARY]
        rest_ref[rows, :] = x[:, BOUNDARY:]
        v_ref[rows, :] = x + over

    run_sweeps(start, finish, lin_ref, over_ref, limits, kh_ref, kl_ref, INNER)


def share_kernel(areas, regions, near, zone_at, weight_ref, edge_ref, rest_ref, share_ref, *across_refs):
    scens = rest_ref.shape[0]
    x = jnp.concatenate([edge_ref[pl.ds(0, scens), :], rest_ref[...]], axis=1)
    sums = weighted_sums(weight_ref[...], x)
    if near:
        share_ref[...] = folded(sums[0:8, :])
        row_id = lax.broadcasted_iota(jnp.int32, (8, scens), 0)
        across = jnp.where(row_id == lax.axis_index("area"), sums[areas + 1 : areas + 2, :], 0.0)
        across_refs[0][...] = folded(jnp.where(row_id == areas, sums[areas : areas + 1, :], across))
        return
    if zone_at is not None:
        me = lax.axis_index("area") * regions + lax.axis_index("region")
        zone = edge_ref[pl.ds(zone_at, 1), pl.ds(0, 1)]
        row_id = lax.broadcasted_iota(jnp.int32, sums.shape, 0)
        sums = sums + jnp.where(row_id == areas * regions + 1 + me, zone, 0.0)
    share_ref[...] = sums[0 : share_ref.shape[0], :]


def append_kernel(scens, kept, zone_at, share_ref, across_ref, edge_ref, side_ref, pair_ref, full_ref, side_out_ref):
    pair = share_ref[...] + across_ref[...]
    rows = pair.shape[0]
    pair_ref[...] = pair
    full_ref[pl.ds(0, scens), :] = edge_ref[pl.ds(0, scens), :]
    full_ref[pl.ds(scens, rows), :] = pair
    if kept:
        full_ref[pl.ds(scens + rows, kept), :] = edge_ref[pl.ds(scens, kept), :]
        full_ref[pl.ds(scens + rows + kept, 1), :] = edge_ref[pl.ds(zone_at, 1), :]
    side_out_ref[...] = side_ref[...]


def live_lines(edge_ref, scens, slots, pieces, p):
    return edge_ref[pl.ds(scens + slots * pieces + 1, 1), pl.ds(p, 1)]


def by_area(values):
    me = lax.axis_index("area")
    out = []
    for k in range(4):
        mask = jnp.bitwise_xor(me, k)
        low = jnp.where(jnp.bitwise_and(mask, 1) == 0, values[0], values[1])
        high = jnp.where(jnp.bitwise_and(mask, 1) == 0, values[2], values[3])
        out.append(jnp.where(mask < 2, low, high))
    return out


def near_sums(scens, pair_ref, opposite_ref, far_ref, close_ref):
    rows = pl.ds(scens, pair_ref.shape[0])
    return unfolded((pair_ref[...] + close_ref[rows, :]) + (opposite_ref[...] + far_ref[rows, :]))


def near_prices(sums, zones, zone):
    price = sums[4:5, :] * SYSTEM_GAIN
    for k in range(4):
        price = price + jnp.where(zones[k] == zone, ZONE_GAIN, 0.0) * sums[k : k + 1, :]
    return price


def prices(shares, zones, total, regions, zone):
    ids = lax.broadcasted_iota(jnp.int32, zones.shape, 0)
    in_region = lax.rem(ids, regions) == lax.axis_index("region")
    gain = jnp.where(in_region & (zones == zone), ZONE_GAIN, 0.0) + SYSTEM_GAIN
    return jnp.sum(gain * shares[0:total, :], axis=0, keepdims=True)


class Mask(int):
    pass


class Plan:
    def __init__(self, areas, regions, scens, slots, pieces):
        self.near = (areas, regions) == (4, 2)
        self.scens, self.pieces = scens, pieces
        self.fold = 8 * (scens // LANES)
        if self.near:
            self.sources = [("area", Mask(2)), ("area", Mask(3)), ("area", Mask(1)), ("region", 1)]
            self.slots_of = [(2, 3), ((1, 0),), ((0, 1),), (4, 5)]
            self.buffer_of = [(2, 1), (1, 2), 0, 0, 3, 3]
            self.early = 1
            return
        self.sources, self.slots_of, self.buffer_of = [], [], [None] * slots
        for p in (2, 3, 0, 1, 4, 5):
            axis, move, _ = SLOTS[p]
            source = (axis, move % (areas if axis == "area" else regions))
            if source not in self.sources:
                self.sources.append(source)
                self.slots_of.append(())
            self.buffer_of[p] = self.sources.index(source)
            self.slots_of[self.buffer_of[p]] += (p,)
        self.early = max(self.buffer_of[2], self.buffer_of[3]) + 1

    def line_row(self, b, p, j):
        back = SLOTS[p][2]
        if self.near:
            back -= {0: 2, 3: 4}.get(b, 0)
        return self.scens + (self.fold if self.near and b in (1, 2) else 0) + back * self.pieces + j

    def zone_row(self, b):
        return self.scens + (self.fold if b in (1, 2) else 0) + 2 * self.pieces


def choice(entry, read):
    if isinstance(entry, int):
        return read(entry)
    even = lax.rem(lax.axis_index("area"), 2) == 0
    return jnp.where(even, read(entry[0]), read(entry[1]))


def coupling_kernel(plan, first, number, own_ref, *refs):
    got, before, coupling_ref = refs[:number], refs[number:-1], refs[-1]
    lines = plan.pieces * LANES
    bus_id = lax.broadcasted_iota(jnp.int32, (BOUNDARY, LANES), 0).astype(F32)
    counts = []
    for b, g in enumerate(got, first):
        met = None
        for entry in plan.slots_of[b]:
            mine = choice(entry, lambda p: own_ref[:, pl.ds(p * lines, lines)])
            there = []
            for j in range(plan.pieces):
                row = choice(entry, lambda p: g[pl.ds(plan.line_row(b, p, j), 1), :])
                there.append(jnp.where(bus_id == row, 1.0, 0.0).astype(BF16))
            pairs = dot_nt(mine, jnp.concatenate(there, axis=1))
            met = pairs if met is None else met + pairs
        counts.append(met)
    counts_high, counts_low = halves(jnp.concatenate(counts, axis=1))
    high, low = halves(jnp.concatenate([g[pl.ds(0, plan.scens), :] for g in got], axis=1))
    out = dot_nt(high, counts_high) + dot_nt(low, counts_high) + dot_nt(high, counts_low)
    for ref in before:
        out = out + ref[...]
    coupling_ref[...] = out


def second_kernel(
    areas, regions, plan, zone_at, lin_ref, coupling_ref, v_ref, kh_ref, kl_ref, cap_ref, edge1_ref, *refs
):
    edge_ref, rest_ref, sums_ref, lin2_ref, over_ref = refs[-5:]
    scens = lin_ref.shape[0]
    zone = edge1_ref[pl.ds(zone_at, 1), pl.ds(0, 1)]
    if plan.near:
        pair_ref, opposite_ref, *got = refs[:-5]
        sums = near_sums(scens, pair_ref, opposite_ref, got[1], got[2])
        zones = by_area([zone] + [got[b][pl.ds(plan.zone_row(b), 1), pl.ds(0, 1)] for b in (2, 0, 1)])
        price = near_prices(sums, zones, zone)
        sums_ref[pl.ds(0, 8), :] = sums
        sums_ref[pl.ds(8, 8), :] = jnp.zeros((8, scens), F32)
        for k in range(4):
            sums_ref[pl.ds(8 + k, 1), :] = jnp.broadcast_to(zones[k], (1, scens))
    else:
        total = areas * regions
        sums = refs[0][...]
        sums_ref[...] = sums
        price = prices(sums, sums[total + 1 : 2 * total + 1, :], total, regions, zone)
    price = jnp.broadcast_to(price, (8, scens)).T[:, 0:1]
    lin2_ref[:, pl.ds(0, BOUNDARY)] = lin_ref[:, pl.ds(0, BOUNDARY)] - price - coupling_ref[...]
    lin2_ref[:, pl.ds(BOUNDARY, BOUNDARY)] = lin_ref[:, pl.ds(BOUNDARY, BOUNDARY)] - price
    limits = cap_ref[...]

    def start(rows):
        clipped, over = clipping(v_ref[rows, :], limits)
        return lin2_ref[rows, :] + (clipped - over), over

    def finish(rows, x, over):
        edge_ref[rows, :] = x[:, :BOUNDARY]
        rest_ref[rows, :] = x[:, BOUNDARY:]

    run_sweeps(start, finish, lin2_ref, over_ref, limits, kh_ref, kl_ref, INNER)


def injection_kernel(edge_ref, rest_ref, injection_ref):
    scens = rest_ref.shape[0]
    injection_ref[0, pl.ds(0, BOUNDARY), :] = edge_ref[pl.ds(0, scens), :].T
    injection_ref[0, pl.ds(BOUNDARY, BOUNDARY), :] = rest_ref[...].T


def table_kernel(plan, own_ref, *refs):
    got = refs[:-2]
    mine_ref, theirs_ref = refs[-2:]
    slots, lines = mine_ref.shape[:2]
    pieces, scens = plan.pieces, plan.scens
    extra = own_ref.shape[0] - scens
    mine = own_ref[pl.ds(scens, extra), :].T
    rows = []
    for p in range(slots):
        rows += [choice(plan.buffer_of[p], lambda b: got[b][pl.ds(plan.line_row(b, p, j), 1), :]) for j in range(pieces)]
        rows.append(jnp.zeros((8 - pieces, LANES), F32))
    theirs = jnp.concatenate(rows, axis=0).T
    bus_id = lax.broadcasted_iota(jnp.int32, (LANES, BOUNDARY), 1).astype(F32)
    line_id = lax.broadcasted_iota(jnp.int32, (LANES, BOUNDARY), 0).astype(F32)
    for p in range(slots):
        number = live_lines(own_ref, scens, slots, pieces, p)
        half = 0.5 * SIGNS[p]
        for j in range(pieces):
            live = jnp.where(line_id + float(j * LANES) < number, half, 0.0)
            at = p * pieces + j
            there = p * 8 + j
            rows = pl.ds(j * LANES, LANES)
            mine_ref[p, rows, :] = jnp.where(bus_id == mine[:, at : at + 1], live, 0.0).astype(BF16)
            theirs_ref[p, rows, :] = jnp.where(bus_id == theirs[:, there : there + 1], -live, 0.0).astype(BF16)


def twice(x):
    return jnp.concatenate([x, x], axis=1)


def own_kernel(table_ref, edge_ref, flow_ref):
    scens = flow_ref.shape[2]
    parts = jnp.concatenate(halves(edge_ref[pl.ds(0, scens), :]), axis=1)
    for p in range(table_ref.shape[0]):
        flow_ref[p] = dot_nt(twice(table_ref[p]), parts)


def write_flows(plan, held, parts, table_ref, own_ref, flow_ref, flow_hbm, sems):
    copies = []
    for i, p in enumerate(held):
        part = choice(plan.buffer_of[p], lambda b: parts[b])
        flow_ref[i] = own_ref[p] + dot_nt(twice(table_ref[p]), part)
        copies.append(pltpu.make_async_copy(flow_ref.at[i], flow_hbm.at[0, p], sems.at[i]))
        copies[-1].start()
    return copies


def parts_of(plan, refs, first):
    return {b: jnp.concatenate(halves(ref[pl.ds(0, plan.scens), :]), axis=1) for b, ref in enumerate(refs, first)}


def early_kernel(plan, table_ref, own_ref, *refs):
    *got, flow_hbm, flow_ref, sems = refs
    parts = parts_of(plan, got, 0)
    for copy in write_flows(plan, (2, 3), parts, table_ref, own_ref, flow_ref, flow_hbm, sems):
        copy.wait()


def final_kernel(areas, regions, plan, number, table_ref, own_ref, sums_ref, *refs):
    got, rest = refs[:number], refs[number:-5]
    flow_hbm, price_ref, flow_ref, sems = refs[-4:]
    parts = parts_of(plan, got, plan.early)
    copies = write_flows(plan, (0, 1, 4, 5), parts, table_ref, own_ref, flow_ref, flow_hbm, sems)
    if plan.near:
        sums = sums_ref[pl.ds(0, 8), :] + near_sums(plan.scens, rest[0], rest[1], got[0], got[1])
        zones = [sums_ref[pl.ds(8 + k, 1), :] for k in range(4)]
        for z in range(ZONES):
            price_ref[pl.ds(z, 1), :] = near_prices(sums, zones, float(z))
    else:
        total = areas * regions
        first = sums_ref[...]
        zones = first[total + 1 : 2 * total + 1, :]
        for z in range(ZONES):
            price_ref[pl.ds(z, 1), :] = prices(first + rest[0][...], zones, total, regions, float(z))
    for copy in copies:
        copy.wait()


def moved(x, axis, by):
    length = lax.axis_size(axis)
    if isinstance(by, Mask):
        return lax.ppermute(x, axis, [(i, i ^ by) for i in range(length)])
    return lax.ppermute(x, axis, [((i + by) % length, i) for i in range(length)])


def body(kkt_inverse, scen_load, capacity, pair_active, tie_counts, line_index, area_zone):
    areas = lax.axis_size("area")
    regions = lax.axis_size("region")
    total = areas * regions
    _, buses, scens = scen_load.shape
    _, slots, lines = line_index.shape
    rest = buses - BOUNDARY
    pieces = lines // LANES
    plan = Plan(areas, regions, scens, slots, pieces)
    near, early = plan.near, plan.early
    zone_at = scens + slots * pieces
    share_rows = -(-(2 * total + 1) // 8) * 8
    weight_rows = 16 if near else -(-share_rows // 16) * 16

    def f32(*shape):
        return jax.ShapeDtypeStruct(shape, F32)

    def bf16(*shape):
        return jax.ShapeDtypeStruct(shape, BF16)

    def cost(flops):
        return pl.CostEstimate(flops=flops, bytes_accessed=0, transcendentals=0)

    def call(kernel, name, out_shape, operands, estimate=None, **more):
        return pl.pallas_call(
            kernel,
            out_shape=out_shape,
            in_specs=more.pop("in_specs", [VMEM] * len(operands)),
            out_specs=more.pop("out_specs", jax.tree.map(lambda _: VMEM, out_shape)),
            compiler_params=PARAMS,
            cost_estimate=estimate and cost(estimate),
            name=name,
            **more,
        )(*operands)

    def exchange(edge, rest, leans, weights, kept):
        held = edge.shape[0] > scens
        shapes = [f32(plan.fold, LANES)] * 2 if near else [f32(share_rows, scens)]
        share, *across = call(
            functools.partial(share_kernel, areas, regions, near, zone_at if held else None),
            "mismatch_shares",
            shapes,
            [weights, edge, rest],
        )
        if not near:
            return [moved(edge, axis, move) for axis, move in plan.sources], [lax.psum(share, ("area", "region"))]
        far, side = leans
        pair, full, side = call(
            functools.partial(append_kernel, scens, kept, zone_at),
            "pair_shares",
            [
                f32(plan.fold, LANES),
                f32(scens + plan.fold + -(-(kept and kept + 1) // 8) * 8, BOUNDARY),
                f32(*side.shape),
            ],
            [share, moved(across[0], "region", 1), edge, side],
        )
        got_side = moved(side, "region", 1)
        opposite = moved(pair, "area", Mask(2))
        got_near = moved(full, "area", Mask(1))
        got_other = moved(full, "area", Mask(3))
        return [moved(far, "area", Mask(2)), got_other, got_near, got_side], [pair, opposite]

    zeros = call(opening_kernel, "opening", f32(8, LANES), [], OPENING)
    lean_rows = -(-(scens + 2 * pieces + 1) // 8) * 8
    leans = [f32(lean_rows, BOUNDARY)] * 2 if near else []
    edge1, *more = call(
        functools.partial(first_kernel, areas, regions, near),
        "first_round",
        [
            f32(-(-(zone_at + 2) // 8) * 8, BOUNDARY),
            *leans,
            f32(scens, rest),
            f32(scens, buses),
            f32(scens, buses),
            bf16(buses, buses),
            bf16(buses, buses),
            bf16(BOUNDARY, slots * lines),
            f32(weight_rows, buses),
        ],
        [
            zeros,
            kkt_inverse,
            scen_load,
            capacity,
            line_index.reshape(slots, 1, lines),
            pair_active,
            tie_counts,
            area_zone,
        ],
        in_specs=[VMEM] * 7 + [SMEM],
        scratch_shapes=[pltpu.VMEM((scens, buses), F32)],
    )
    leans1, (rest1, state, lin, kh, kl, own, weights) = more[: len(leans)], more[len(leans) :]
    got1, sums1 = exchange(edge1, rest1, leans1, weights, 2 * pieces)
    coupling = call(
        functools.partial(coupling_kernel, plan, 0, early),
        "coupling",
        f32(scens, BOUNDARY),
        [own, *got1[:early]],
        BIG,
    )
    coupling = call(
        functools.partial(coupling_kernel, plan, early, len(got1) - early),
        "coupling",
        f32(scens, BOUNDARY),
        [own, *got1[early:], coupling],
        BIG,
    )
    edge2, rest2, first = call(
        functools.partial(second_kernel, areas, regions, plan, zone_at),
        "second_round",
        [f32(scens, BOUNDARY), f32(scens, rest), f32(16 if near else share_rows, scens)],
        [lin, coupling, state, kh, kl, capacity, edge1, *sums1, *(got1 if near else [])],
        scratch_shapes=[pltpu.VMEM((scens, buses), F32)] * 2,
    )
    got2, sums2 = exchange(edge2, rest2, [edge2] * 2, weights, 0)
    injection = call(injection_kernel, "injection", f32(1, buses, scens), [edge2, rest2])
    mine, theirs = call(
        functools.partial(table_kernel, plan),
        "line_table",
        [bf16(slots, lines, BOUNDARY)] * 2,
        [edge1, *got1],
    )
    own_flow = call(own_kernel, "own_flows", f32(slots, lines, scens), [mine, edge2])
    operands = [theirs, own_flow, *got2[:early]]
    flow = call(
        functools.partial(early_kernel, plan),
        "tie_flows_early",
        f32(1, slots, lines, scens),
        operands,
        BIG,
        out_specs=HBM,
        scratch_shapes=[pltpu.VMEM((2, lines, scens), F32), pltpu.SemaphoreType.DMA((2,))],
    )
    operands = [theirs, own_flow, first, *got2[early:], *sums2, flow]
    flow, price = call(
        functools.partial(final_kernel, areas, regions, plan, len(got2) - early),
        "tie_flows",
        (f32(1, slots, lines, scens), f32(ZONES, scens)),
        operands,
        BIG,
        in_specs=[VMEM] * (len(operands) - 1) + [HBM],
        out_specs=(HBM, VMEM),
        input_output_aliases={len(operands) - 1: 0},
        scratch_shapes=[pltpu.VMEM((slots - 2, lines, scens), F32), pltpu.SemaphoreType.DMA((slots - 2,))],
    )
    return injection, flow, price


def solution(mesh):
    placed = (
        P(("area", "region"), None, None),
        P(("area", "region"), None, ("group", "scen")),
        P(("area", "region"), None),
        P(("area", "region"), None),
        P(("area", "region"), None),
        P(("area", "region"), None, None),
        P(("area", "region")),
    )
    return jax.shard_map(
        body,
        mesh=mesh,
        in_specs=placed,
        out_specs=(
            P(("area", "region"), None, ("group", "scen")),
            P(("area", "region"), None, None, ("group", "scen")),
            P("region", ("group", "scen")),
        ),
        check_vma=False,
    )
```

```python
import functools

import jax
import jax.numpy as jnp
from jax import lax
from jax.experimental import pallas as pl
from jax.experimental.pallas import tpu as pltpu
from jax.sharding import PartitionSpec as P

ZONES = 4
INNER = 24
BOUNDARY = 128
LANES = 128
ZONE_GAIN = 0.004
SYSTEM_GAIN = 0.001
SLOTS = (
    ("area", 1, 1),
    ("area", -1, 0),
    ("area", 2, 3),
    ("area", -2, 2),
    ("region", 1, 5),
    ("region", -1, 4),
)
SIGNS = (1.0, -1.0, 1.0, -1.0, 1.0, -1.0)
CHAIN_ROWS = 32
UNROLL = 4
BIG = 4 * 10**9
OPENING = 10**11

F32 = jnp.float32
BF16 = jnp.bfloat16
VMEM = pl.BlockSpec(memory_space=pltpu.VMEM)
SMEM = pl.BlockSpec(memory_space=pltpu.SMEM)
HBM = pl.BlockSpec(memory_space=pltpu.HBM)
PARAMS = pltpu.CompilerParams(vmem_limit_bytes=40 * 2**20)


def dot(a, b):
    return jnp.dot(a, b, preferred_element_type=F32)


def dot_nt(a, b):
    return lax.dot_general(a, b, (((1,), (1,)), ((), ())), preferred_element_type=F32)


def halves(x):
    high = x.astype(BF16)
    return high, (x - high.astype(F32)).astype(BF16)


def thirds(x):
    high = x.astype(BF16)
    rest = x - high.astype(F32)
    middle = rest.astype(BF16)
    return high, middle, (rest - middle.astype(F32)).astype(BF16)


def clipping(v, limits):
    clipped = jnp.clip(v, -limits, limits)
    return clipped, v - clipped


def run_sweeps(start, finish, lin_ref, over_ref, limits, kh_ref, kl_ref, count):
    scens, buses = lin_ref.shape
    chains = scens // CHAIN_ROWS

    def scoped(*accumulators):
        highs, lows = accumulators[:chains], accumulators[chains:]
        pltpu.matmul_push_rhs(kh_ref[...], 0, 0)
        pltpu.matmul_push_rhs(kl_ref[...], 0, 1)

        def issue(i, x, load=None):
            high, low = halves(x)
            pltpu.matmul_acc_lhs(highs[i], high, load)
            pltpu.matmul_acc_lhs(highs[i], low)
            pltpu.matmul_acc_lhs(lows[i], high, load)

        def rows_of(i):
            return pl.ds(i * CHAIN_ROWS, CHAIN_ROWS)

        def taken(i):
            return pltpu.matmul_pop(highs[i]) + pltpu.matmul_pop(lows[i])

        for i in range(chains):
            x, over = start(rows_of(i))
            over_ref[rows_of(i), :] = over
            issue(i, x, 0 if i == 0 else None)

        def sweep(_, carry):
            for i in range(chains):
                rows = rows_of(i)
                clipped, over = clipping(taken(i) + over_ref[rows, :], limits)
                over_ref[rows, :] = over
                issue(i, lin_ref[rows, :] + (clipped - over))
            return carry

        lax.fori_loop(0, count - 1, sweep, 0, unroll=UNROLL)
        for i in range(chains):
            finish(rows_of(i), taken(i), over_ref[rows_of(i), :])

    pl.run_scoped(
        scoped,
        *[pltpu.ACC(0)((CHAIN_ROWS, buses), F32)] * chains,
        *[pltpu.ACC(1)((CHAIN_ROWS, buses), F32)] * chains,
    )


def line_tables(areas, regions, slots, pieces, near, idx_row, number, own_ref, rows):
    me_area, me_region = lax.axis_index("area"), lax.axis_index("region")
    here = me_area if near else me_area * regions + me_region
    width = -(-rows // LANES) * LANES
    row_id = lax.broadcasted_iota(jnp.int32, (1, width), 1)
    line_id = lax.broadcasted_iota(jnp.int32, (1, LANES), 1).astype(F32)
    bus_id = lax.broadcasted_iota(jnp.int32, (BOUNDARY, LANES), 0).astype(F32)
    weights = jnp.zeros((BOUNDARY, width), F32)
    for p in range(slots):
        axis, move, _ = SLOTS[p]
        if axis == "area":
            other = lax.rem(me_area + move % areas, areas)
            there = other if near else other * regions + me_region
        else:
            there = areas + 1 if near else me_area * regions + lax.rem(me_region + move % regions, regions)
        coefficient = jnp.where(row_id == there, 0.5, 0.0) - jnp.where(row_id == here, 0.5, 0.0)
        met = None
        for j in range(pieces):
            row = jnp.where(line_id + float(j * LANES) < number(p), idx_row(p, j), -1.0)
            onehot = jnp.where(bus_id == row, 1.0, 0.0)
            own_ref[:, pl.ds((p * pieces + j) * LANES, LANES)] = onehot.astype(BF16)
            met = onehot if met is None else met + onehot
        weights = weights + jnp.sum(met, axis=1, keepdims=True) * coefficient
    last = areas if near else areas * regions
    mine = jnp.where((row_id == here) | (row_id == last), 1.0, 0.0)
    weights = jnp.concatenate([weights + mine, jnp.broadcast_to(mine, (BOUNDARY, width))], axis=0)
    return weights.T[0:rows, :]


def weighted_sums(weights, x):
    wh, wl = halves(weights)
    xh, xm, xl = thirds(x)
    return dot_nt(wh, xh) + (dot_nt(wh, xm) + dot_nt(wl, xh)) + (dot_nt(wh, xl) + dot_nt(wl, xm))


def folded(x):
    return jnp.concatenate([x[:, j : j + LANES] for j in range(0, x.shape[1], LANES)], axis=0)


def unfolded(x):
    return jnp.concatenate([x[j : j + 8, :] for j in range(0, x.shape[0], 8)], axis=1)


def opening_kernel(zeros_ref):
    zeros_ref[...] = jnp.zeros(zeros_ref.shape, F32)


def first_kernel(
    areas, regions, near, zeros_ref, k_ref, load_ref, cap_ref, idx_ref, active_ref, count_ref, zone_ref, *refs
):
    edge_ref, *lean_refs = refs[:-8]
    rest_ref, v_ref, lin_ref, kh_ref, kl_ref, own_ref, weight_ref, over_ref = refs[-8:]
    scens = lin_ref.shape[0]
    slots, _, lines = idx_ref.shape
    pieces = lines // LANES
    numbers = jnp.where(active_ref[...] > 0, count_ref[...], 0).astype(F32)
    zone = jnp.full((1, LANES), zone_ref[0].astype(F32))

    def idx_row(p, j):
        return idx_ref[p, :, pl.ds(j * LANES, LANES)].astype(F32)

    for ref, held in ((edge_ref, range(slots)), *zip(lean_refs, ((2, 3), (4, 5)))):
        ref[pl.ds(ref.shape[0] - 8, 8), :] = zeros_ref[...]
        at = scens
        for p in held:
            for j in range(pieces):
                ref[pl.ds(at, 1), :] = idx_row(p, j)
                at += 1
        ref[pl.ds(at, 1), :] = zone
    edge_ref[pl.ds(scens + slots * pieces + 1, 1), pl.ds(0, slots)] = numbers
    weight_ref[...] = line_tables(
        areas, regions, slots, pieces, near, idx_row, lambda p: numbers[:, p : p + 1], own_ref, weight_ref.shape[0]
    )
    high, low = halves(k_ref[0].T)
    kh_ref[...] = high
    kl_ref[...] = low
    lin_ref[...] = load_ref[0].T
    limits = cap_ref[...]

    def start(rows):
        return lin_ref[rows, :], jnp.zeros((CHAIN_ROWS, lin_ref.shape[1]), F32)

    def finish(rows, x, over):
        for ref in (edge_ref, *lean_refs):
            ref[rows, :] = x[:, :BOUNDARY]
        rest_ref[rows, :] = x[:, BOUNDARY:]
        v_ref[rows, :] = x + over

    run_sweeps(start, finish, lin_ref, over_ref, limits, kh_ref, kl_ref, INNER)


def share_kernel(areas, regions, near, zone_at, weight_ref, edge_ref, rest_ref, share_ref, *across_refs):
    scens = rest_ref.shape[0]
    x = jnp.concatenate([edge_ref[pl.ds(0, scens), :], rest_ref[...]], axis=1)
    sums = weighted_sums(weight_ref[...], x)
    if near:
        share_ref[...] = folded(sums[0:8, :])
        row_id = lax.broadcasted_iota(jnp.int32, (8, scens), 0)
        across = jnp.where(row_id == lax.axis_index("area"), sums[areas + 1 : areas + 2, :], 0.0)
        across_refs[0][...] = folded(jnp.where(row_id == areas, sums[areas : areas + 1, :], across))
        return
    if zone_at is not None:
        me = lax.axis_index("area") * regions + lax.axis_index("region")
        zone = edge_ref[pl.ds(zone_at, 1), pl.ds(0, 1)]
        row_id = lax.broadcasted_iota(jnp.int32, sums.shape, 0)
        sums = sums + jnp.where(row_id == areas * regions + 1 + me, zone, 0.0)
    share_ref[...] = sums[0 : share_ref.shape[0], :]


def append_kernel(scens, kept, zone_at, share_ref, across_ref, edge_ref, side_ref, pair_ref, full_ref, side_out_ref):
    pair = share_ref[...] + across_ref[...]
    rows = pair.shape[0]
    pair_ref[...] = pair
    full_ref[pl.ds(0, scens), :] = edge_ref[pl.ds(0, scens), :]
    full_ref[pl.ds(scens, rows), :] = pair
    if kept:
        full_ref[pl.ds(scens + rows, kept), :] = edge_ref[pl.ds(scens, kept), :]
        full_ref[pl.ds(scens + rows + kept, 1), :] = edge_ref[pl.ds(zone_at, 1), :]
    side_out_ref[...] = side_ref[...]


def live_lines(edge_ref, scens, slots, pieces, p):
    return edge_ref[pl.ds(scens + slots * pieces + 1, 1), pl.ds(p, 1)]


def by_area(values):
    me = lax.axis_index("area")
    out = []
    for k in range(4):
        mask = jnp.bitwise_xor(me, k)
        low = jnp.where(jnp.bitwise_and(mask, 1) == 0, values[0], values[1])
        high = jnp.where(jnp.bitwise_and(mask, 1) == 0, values[2], values[3])
        out.append(jnp.where(mask < 2, low, high))
    return out


def near_sums(scens, pair_ref, opposite_ref, far_ref, close_ref):
    rows = pl.ds(scens, pair_ref.shape[0])
    return unfolded((pair_ref[...] + close_ref[rows, :]) + (opposite_ref[...] + far_ref[rows, :]))


def near_prices(sums, zones, zone):
    price = sums[4:5, :] * SYSTEM_GAIN
    for k in range(4):
        price = price + jnp.where(zones[k] == zone, ZONE_GAIN, 0.0) * sums[k : k + 1, :]
    return price


def prices(shares, zones, total, regions, zone):
    ids = lax.broadcasted_iota(jnp.int32, zones.shape, 0)
    in_region = lax.rem(ids, regions) == lax.axis_index("region")
    gain = jnp.where(in_region & (zones == zone), ZONE_GAIN, 0.0) + SYSTEM_GAIN
    return jnp.sum(gain * shares[0:total, :], axis=0, keepdims=True)


class Mask(int):
    pass


class Plan:
    def __init__(self, areas, regions, scens, slots, pieces):
        self.near = (areas, regions) == (4, 2)
        self.scens, self.pieces = scens, pieces
        self.fold = 8 * (scens // LANES)
        if self.near:
            self.sources = [("area", Mask(2)), ("area", Mask(3)), ("area", Mask(1)), ("region", 1)]
            self.slots_of = [(2, 3), ((1, 0),), ((0, 1),), (4, 5)]
            self.buffer_of = [(2, 1), (1, 2), 0, 0, 3, 3]
            self.arrivals = [(0,), (1, 2, 3)]
            self.last = (1, 2, 3)
            return
        self.sources, self.slots_of, self.buffer_of = [], [], [None] * slots
        for p in (2, 3, 0, 1, 4, 5):
            axis, move, _ = SLOTS[p]
            source = (axis, move % (areas if axis == "area" else regions))
            if source not in self.sources:
                self.sources.append(source)
                self.slots_of.append(())
            self.buffer_of[p] = self.sources.index(source)
            self.slots_of[self.buffer_of[p]] += (p,)
        self.arrivals = [tuple(range(len(self.sources)))]
        self.last = self.arrivals[0]

    def line_row(self, b, p, j):
        back = SLOTS[p][2]
        if self.near:
            back -= {0: 2, 3: 4}.get(b, 0)
        return self.scens + (self.fold if self.near and b in (1, 2) else 0) + back * self.pieces + j

    def zone_row(self, b):
        return self.scens + (self.fold if b in (1, 2) else 0) + 2 * self.pieces


def choice(entry, read):
    if isinstance(entry, int):
        return read(entry)
    even = lax.rem(lax.axis_index("area"), 2) == 0
    return jnp.where(even, read(entry[0]), read(entry[1]))


def coupling_kernel(plan, held, own_ref, *refs):
    got, before, coupling_ref = refs[: len(held)], refs[len(held) : -1], refs[-1]
    lines = plan.pieces * LANES
    bus_id = lax.broadcasted_iota(jnp.int32, (BOUNDARY, LANES), 0).astype(F32)
    counts = []
    for b, g in zip(held, got):
        met = None
        for entry in plan.slots_of[b]:
            mine = choice(entry, lambda p: own_ref[:, pl.ds(p * lines, lines)])
            there = []
            for j in range(plan.pieces):
                row = choice(entry, lambda p: g[pl.ds(plan.line_row(b, p, j), 1), :])
                there.append(jnp.where(bus_id == row, 1.0, 0.0).astype(BF16))
            pairs = dot_nt(mine, jnp.concatenate(there, axis=1))
            met = pairs if met is None else met + pairs
        counts.append(met)
    counts_high, counts_low = halves(jnp.concatenate(counts, axis=1))
    high, low = halves(jnp.concatenate([g[pl.ds(0, plan.scens), :] for g in got], axis=1))
    out = dot_nt(high, counts_high) + dot_nt(low, counts_high) + dot_nt(high, counts_low)
    for ref in before:
        out = out + ref[...]
    coupling_ref[...] = out


def second_kernel(
    areas, regions, plan, zone_at, *refs
):
    *front, lin_ref, coupling_ref, v_ref, kh_ref, kl_ref, cap_ref, edge1_ref = refs[:-6]
    refs = (*front, *refs[-6:])
    edge_ref, rest_ref, sums_ref, lin2_ref, over_ref = refs[-5:]
    scens = lin_ref.shape[0]
    zone = edge1_ref[pl.ds(zone_at, 1), pl.ds(0, 1)]
    if plan.near:
        pair_ref, opposite_ref, *got = refs[:-6]
        sums = near_sums(scens, pair_ref, opposite_ref, got[1], got[2])
        zones = by_area([zone] + [got[b][pl.ds(plan.zone_row(b), 1), pl.ds(0, 1)] for b in (2, 0, 1)])
        price = near_prices(sums, zones, zone)
        sums_ref[pl.ds(0, 8), :] = sums
        sums_ref[pl.ds(8, 8), :] = jnp.zeros((8, scens), F32)
        for k in range(4):
            sums_ref[pl.ds(8 + k, 1), :] = jnp.broadcast_to(zones[k], (1, scens))
    else:
        total = areas * regions
        sums = refs[0][...]
        sums_ref[...] = sums
        price = prices(sums, sums[total + 1 : 2 * total + 1, :], total, regions, zone)
    price = jnp.broadcast_to(price, (8, scens)).T[:, 0:1]
    lin2_ref[:, pl.ds(0, BOUNDARY)] = lin_ref[:, pl.ds(0, BOUNDARY)] - price - coupling_ref[...]
    lin2_ref[:, pl.ds(BOUNDARY, BOUNDARY)] = lin_ref[:, pl.ds(BOUNDARY, BOUNDARY)] - price
    limits = cap_ref[...]

    def start(rows):
        clipped, over = clipping(v_ref[rows, :], limits)
        return lin2_ref[rows, :] + (clipped - over), over

    def finish(rows, x, over):
        edge_ref[rows, :] = x[:, :BOUNDARY]
        rest_ref[rows, :] = x[:, BOUNDARY:]

    run_sweeps(start, finish, lin2_ref, over_ref, limits, kh_ref, kl_ref, INNER)


def injection_kernel(edge_ref, rest_ref, injection_ref):
    scens = rest_ref.shape[0]
    injection_ref[0, pl.ds(0, BOUNDARY), :] = edge_ref[pl.ds(0, scens), :].T
    injection_ref[0, pl.ds(BOUNDARY, BOUNDARY), :] = rest_ref[...].T


def own_table_kernel(plan, own_ref, table_ref):
    pieces, scens = plan.pieces, plan.scens
    mine = own_ref[pl.ds(scens, own_ref.shape[0] - scens), :].T
    fill_table(plan, own_ref, table_ref, 0.5, lambda p, j: mine[:, p * pieces + j : p * pieces + j + 1])


def fill_table(plan, own_ref, table_ref, half, column):
    slots, pieces, scens = table_ref.shape[0], plan.pieces, plan.scens
    bus_id = lax.broadcasted_iota(jnp.int32, (LANES, BOUNDARY), 1).astype(F32)
    line_id = lax.broadcasted_iota(jnp.int32, (LANES, BOUNDARY), 0).astype(F32)
    for p in range(slots):
        number = live_lines(own_ref, scens, slots, pieces, p)
        for j in range(pieces):
            live = jnp.where(line_id + float(j * LANES) < number, half * SIGNS[p], 0.0)
            table_ref[p, pl.ds(j * LANES, LANES), :] = jnp.where(bus_id == column(p, j), live, 0.0).astype(BF16)


def table_kernel(plan, own_ref, *refs):
    got = refs[:-1]
    table_ref = refs[-1]
    slots, pieces = table_ref.shape[0], plan.pieces
    rows = []
    for p in range(slots):
        rows += [choice(plan.buffer_of[p], lambda b: got[b][pl.ds(plan.line_row(b, p, j), 1), :]) for j in range(pieces)]
        rows.append(jnp.zeros((8 - pieces, LANES), F32))
    theirs = jnp.concatenate(rows, axis=0).T
    fill_table(plan, own_ref, table_ref, -0.5, lambda p, j: theirs[:, p * 8 + j : p * 8 + j + 1])


def twice(x):
    return jnp.concatenate([x, x], axis=1)


def own_kernel(table_ref, edge_ref, flow_ref):
    scens = flow_ref.shape[2]
    parts = jnp.concatenate(halves(edge_ref[pl.ds(0, scens), :]), axis=1)
    for p in range(table_ref.shape[0]):
        flow_ref[p] = dot_nt(twice(table_ref[p]), parts)


def write_flows(plan, held, parts, table_ref, own_ref, flow_ref, flow_hbm, sems):
    copies = []
    for i, p in enumerate(held):
        part = choice(plan.buffer_of[p], lambda b: parts[b])
        flow_ref[i] = own_ref[p] + dot_nt(twice(table_ref[p]), part)
        copies.append(pltpu.make_async_copy(flow_ref.at[i], flow_hbm.at[0, p], sems.at[i]))
        copies[-1].start()
    return copies


def parts_of(plan, refs, held):
    return {b: jnp.concatenate(halves(ref[pl.ds(0, plan.scens), :]), axis=1) for b, ref in zip(held, refs)}


def parts_kernel(ref, part_ref):
    part_ref[...] = jnp.concatenate(halves(ref[pl.ds(0, part_ref.shape[0]), :]), axis=1)


def final_kernel(plan, table_ref, own_ref, *refs):
    *got, flow_hbm, done_ref, flow_ref, sems = refs
    if plan.near:
        parts = {0: got[0][...]}
        got = got[1:]
    else:
        parts = {}
    parts.update(parts_of(plan, got, plan.last))
    copies = write_flows(plan, (2, 3, 4, 5, 0, 1), parts, table_ref, own_ref, flow_ref, flow_hbm, sems)
    done_ref[...] = jnp.zeros(done_ref.shape, F32)
    for copy in copies:
        copy.wait()


def price_kernel(areas, regions, near, first_ref, done_ref, *refs):
    *rest, price_ref = refs
    if near:
        own, one, two, three = rest
        sums = first_ref[pl.ds(0, 8), :] + unfolded((own[...] + one[...]) + (two[...] + three[...]))
        zones = [first_ref[pl.ds(8 + k, 1), :] for k in range(4)]
        for z in range(ZONES):
            price_ref[pl.ds(z, 1), :] = near_prices(sums, zones, float(z))
        return
    total = areas * regions
    first = first_ref[...]
    zones = first[total + 1 : 2 * total + 1, :]
    for z in range(ZONES):
        price_ref[pl.ds(z, 1), :] = prices(first + rest[0][...], zones, total, regions, float(z))


def moved(x, axis, by):
    length = lax.axis_size(axis)
    if isinstance(by, Mask):
        return lax.ppermute(x, axis, [(i, i ^ by) for i in range(length)])
    return lax.ppermute(x, axis, [((i + by) % length, i) for i in range(length)])


def body(kkt_inverse, scen_load, capacity, pair_active, tie_counts, line_index, area_zone):
    areas = lax.axis_size("area")
    regions = lax.axis_size("region")
    total = areas * regions
    _, buses, scens = scen_load.shape
    _, slots, lines = line_index.shape
    rest = buses - BOUNDARY
    pieces = lines // LANES
    plan = Plan(areas, regions, scens, slots, pieces)
    near = plan.near
    zone_at = scens + slots * pieces
    share_rows = -(-(2 * total + 1) // 8) * 8
    weight_rows = 16 if near else -(-share_rows // 16) * 16

    def f32(*shape):
        return jax.ShapeDtypeStruct(shape, F32)

    def bf16(*shape):
        return jax.ShapeDtypeStruct(shape, BF16)

    def cost(flops):
        return pl.CostEstimate(flops=flops, bytes_accessed=0, transcendentals=0)

    def call(kernel, name, out_shape, operands, estimate=None, **more):
        return pl.pallas_call(
            kernel,
            out_shape=out_shape,
            in_specs=more.pop("in_specs", [VMEM] * len(operands)),
            out_specs=more.pop("out_specs", jax.tree.map(lambda _: VMEM, out_shape)),
            compiler_params=PARAMS,
            cost_estimate=estimate and cost(estimate),
            name=name,
            **more,
        )(*operands)

    def exchange_last(edge, rest, weights):
        got = [moved(edge, axis, move) for axis, move in plan.sources[::-1]][::-1]
        share, across = call(
            functools.partial(share_kernel, areas, regions, near, None),
            "mismatch_shares",
            [f32(plan.fold, LANES)] * 2,
            [weights, edge, rest],
        )
        pair = share + moved(across, "region", 1)
        return got, [pair, *(moved(pair, "area", Mask(mask)) for mask in (1, 2, 3))]

    def exchange(edge, rest, leans, weights, kept):
        held = edge.shape[0] > scens
        shapes = [f32(plan.fold, LANES)] * 2 if near else [f32(share_rows, scens)]
        share, *across = call(
            functools.partial(share_kernel, areas, regions, near, zone_at if held else None),
            "mismatch_shares",
            shapes,
            [weights, edge, rest],
        )
        if not near:
            return [moved(edge, axis, move) for axis, move in plan.sources], [lax.psum(share, ("area", "region"))]
        far, side = leans
        pair, full, side = call(
            functools.partial(append_kernel, scens, kept, zone_at),
            "pair_shares",
            [
                f32(plan.fold, LANES),
                f32(scens + plan.fold + -(-(kept and kept + 1) // 8) * 8, BOUNDARY),
                f32(*side.shape),
            ],
            [share, moved(across[0], "region", 1), edge, side],
        )
        got_side = moved(side, "region", 1)
        opposite = moved(pair, "area", Mask(2))
        got_near = moved(full, "area", Mask(1))
        got_other = moved(full, "area", Mask(3))
        return [moved(far, "area", Mask(2)), got_other, got_near, got_side], [pair, opposite]

    zeros = call(opening_kernel, "opening", f32(8, LANES), [], OPENING)
    lean_rows = -(-(scens + 2 * pieces + 1) // 8) * 8
    leans = [f32(lean_rows, BOUNDARY)] * 2 if near else []
    edge1, *more = call(
        functools.partial(first_kernel, areas, regions, near),
        "first_round",
        [
            f32(-(-(zone_at + 2) // 8) * 8, BOUNDARY),
            *leans,
            f32(scens, rest),
            f32(scens, buses),
            f32(scens, buses),
            bf16(buses, buses),
            bf16(buses, buses),
            bf16(BOUNDARY, slots * lines),
            f32(weight_rows, buses),
        ],
        [
            zeros,
            kkt_inverse,
            scen_load,
            capacity,
            line_index.reshape(slots, 1, lines),
            pair_active,
            tie_counts,
            area_zone,
        ],
        in_specs=[VMEM] * 7 + [SMEM],
        scratch_shapes=[pltpu.VMEM((scens, buses), F32)],
    )
    leans1, (rest1, state, lin, kh, kl, own, weights) = more[: len(leans)], more[len(leans) :]
    got1, sums1 = exchange(edge1, rest1, leans1, weights, 2 * pieces)
    coupling = []
    for held in plan.arrivals:
        coupling = [
            call(
                functools.partial(coupling_kernel, plan, held),
                "coupling",
                f32(scens, BOUNDARY),
                [own, *(got1[b] for b in held), *coupling],
                BIG,
            )
        ]
    mine = call(functools.partial(own_table_kernel, plan), "own_table", bf16(slots, lines, BOUNDARY), [edge1])
    edge2, rest2, first = call(
        functools.partial(second_kernel, areas, regions, plan, zone_at),
        "second_round",
        [f32(scens, BOUNDARY), f32(scens, rest), f32(16 if near else share_rows, scens)],
        [*sums1, *(got1 if near else []), lin, *coupling, state, kh, kl, capacity, edge1, mine],
        scratch_shapes=[pltpu.VMEM((scens, buses), F32)] * 2,
    )
    if near:
        got2, sums2 = exchange_last(edge2, rest2, weights)
    else:
        got2, sums2 = exchange(edge2, rest2, [], weights, 0)
    injection = call(injection_kernel, "injection", f32(1, buses, scens), [edge2, rest2])
    theirs = call(functools.partial(table_kernel, plan), "line_table", bf16(slots, lines, BOUNDARY), [edge1, *got1])
    own_flow = call(own_kernel, "own_flows", f32(slots, lines, scens), [mine, edge2])
    operands = got2
    if near:
        far = call(parts_kernel, "injection_parts", bf16(scens, 2 * BOUNDARY), got2[:1], BIG)
        operands = [far, *(got2[b] for b in plan.last)]
    flow, done = call(
        functools.partial(final_kernel, plan),
        "tie_flows",
        (f32(1, slots, lines, scens), f32(8, LANES)),
        [theirs, own_flow, *operands],
        BIG,
        out_specs=(HBM, VMEM),
        scratch_shapes=[pltpu.VMEM((slots, lines, scens), F32), pltpu.SemaphoreType.DMA((slots,))],
    )
    price = call(
        functools.partial(price_kernel, areas, regions, near),
        "zone_prices",
        f32(ZONES, scens),
        [first, done, *sums2],
    )
    return injection, flow, price


def solution(mesh):
    placed = (
        P(("area", "region"), None, None),
        P(("area", "region"), None, ("group", "scen")),
        P(("area", "region"), None),
        P(("area", "region"), None),
        P(("area", "region"), None),
        P(("area", "region"), None, None),
        P(("area", "region")),
    )
    return jax.shard_map(
        body,
        mesh=mesh,
        in_specs=placed,
        out_specs=(
            P(("area", "region"), None, ("group", "scen")),
            P(("area", "region"), None, None, ("group", "scen")),
            P("region", ("group", "scen")),
        ),
        check_vma=False,
    )
```

```python
import functools

import jax
import jax.numpy as jnp
from jax import lax
from jax.experimental import pallas as pl
from jax.experimental.pallas import tpu as pltpu
from jax.sharding import PartitionSpec as P

ZONES = 4
INNER = 24
BOUNDARY = 128
LANES = 128
ZONE_GAIN = 0.004
SYSTEM_GAIN = 0.001
SLOTS = (
    ("area", 1, 1),
    ("area", -1, 0),
    ("area", 2, 3),
    ("area", -2, 2),
    ("region", 1, 5),
    ("region", -1, 4),
)
SIGNS = (1.0, -1.0, 1.0, -1.0, 1.0, -1.0)
CHAIN_ROWS = 32
UNROLL = 4
BIG = 4 * 10**9
OPENING = 10**11

F32 = jnp.float32
BF16 = jnp.bfloat16
VMEM = pl.BlockSpec(memory_space=pltpu.VMEM)
SMEM = pl.BlockSpec(memory_space=pltpu.SMEM)
HBM = pl.BlockSpec(memory_space=pltpu.HBM)
PARAMS = pltpu.CompilerParams(vmem_limit_bytes=40 * 2**20)


def dot(a, b):
    return jnp.dot(a, b, preferred_element_type=F32)


def dot_nt(a, b):
    return lax.dot_general(a, b, (((1,), (1,)), ((), ())), preferred_element_type=F32)


def halves(x):
    high = x.astype(BF16)
    return high, (x - high.astype(F32)).astype(BF16)


def thirds(x):
    high = x.astype(BF16)
    rest = x - high.astype(F32)
    middle = rest.astype(BF16)
    return high, middle, (rest - middle.astype(F32)).astype(BF16)


def clipping(v, limits):
    clipped = jnp.clip(v, -limits, limits)
    return clipped, v - clipped


def run_sweeps(start, finish, lin_ref, over_ref, limits, kh_ref, kl_ref, count):
    scens, buses = lin_ref.shape
    chains = scens // CHAIN_ROWS

    def scoped(*accumulators):
        highs, lows = accumulators[:chains], accumulators[chains:]
        pltpu.matmul_push_rhs(kh_ref[...], 0, 0)
        pltpu.matmul_push_rhs(kl_ref[...], 0, 1)

        def issue(i, x, load=None):
            high, low = halves(x)
            pltpu.matmul_acc_lhs(highs[i], high, load)
            pltpu.matmul_acc_lhs(highs[i], low)
            pltpu.matmul_acc_lhs(lows[i], high, load)

        def rows_of(i):
            return pl.ds(i * CHAIN_ROWS, CHAIN_ROWS)

        def taken(i):
            return pltpu.matmul_pop(highs[i]) + pltpu.matmul_pop(lows[i])

        for i in range(chains):
            x, over = start(rows_of(i))
            over_ref[rows_of(i), :] = over
            issue(i, x, 0 if i == 0 else None)

        def sweep(_, carry):
            for i in range(chains):
                rows = rows_of(i)
                clipped, over = clipping(taken(i) + over_ref[rows, :], limits)
                over_ref[rows, :] = over
                issue(i, lin_ref[rows, :] + (clipped - over))
            return carry

        lax.fori_loop(0, count - 1, sweep, 0, unroll=UNROLL)
        for i in range(chains):
            finish(rows_of(i), taken(i), over_ref[rows_of(i), :])

    pl.run_scoped(
        scoped,
        *[pltpu.ACC(0)((CHAIN_ROWS, buses), F32)] * chains,
        *[pltpu.ACC(1)((CHAIN_ROWS, buses), F32)] * chains,
    )


def line_tables(areas, regions, slots, pieces, near, idx_row, number, own_ref, rows):
    me_area, me_region = lax.axis_index("area"), lax.axis_index("region")
    here = me_area if near else me_area * regions + me_region
    width = -(-rows // LANES) * LANES
    row_id = lax.broadcasted_iota(jnp.int32, (1, width), 1)
    line_id = lax.broadcasted_iota(jnp.int32, (1, LANES), 1).astype(F32)
    bus_id = lax.broadcasted_iota(jnp.int32, (BOUNDARY, LANES), 0).astype(F32)
    weights = jnp.zeros((BOUNDARY, width), F32)
    for p in range(slots):
        axis, move, _ = SLOTS[p]
        if axis == "area":
            other = lax.rem(me_area + move % areas, areas)
            there = other if near else other * regions + me_region
        else:
            there = areas + 1 if near else me_area * regions + lax.rem(me_region + move % regions, regions)
        coefficient = jnp.where(row_id == there, 0.5, 0.0) - jnp.where(row_id == here, 0.5, 0.0)
        met = None
        for j in range(pieces):
            row = jnp.where(line_id + float(j * LANES) < number(p), idx_row(p, j), -1.0)
            onehot = jnp.where(bus_id == row, 1.0, 0.0)
            own_ref[:, pl.ds((p * pieces + j) * LANES, LANES)] = onehot.astype(BF16)
            met = onehot if met is None else met + onehot
        weights = weights + jnp.sum(met, axis=1, keepdims=True) * coefficient
    last = areas if near else areas * regions
    mine = jnp.where((row_id == here) | (row_id == last), 1.0, 0.0)
    weights = jnp.concatenate([weights + mine, jnp.broadcast_to(mine, (BOUNDARY, width))], axis=0)
    return weights.T[0:rows, :]


def weighted_sums(weights, x):
    wh, wl = halves(weights)
    xh, xm, xl = thirds(x)
    return dot_nt(wh, xh) + (dot_nt(wh, xm) + dot_nt(wl, xh)) + (dot_nt(wh, xl) + dot_nt(wl, xm))


def folded(x):
    return jnp.concatenate([x[:, j : j + LANES] for j in range(0, x.shape[1], LANES)], axis=0)


def unfolded(x):
    return jnp.concatenate([x[j : j + 8, :] for j in range(0, x.shape[0], 8)], axis=1)


def opening_kernel(zeros_ref):
    zeros_ref[...] = jnp.zeros(zeros_ref.shape, F32)


def lines_kernel(areas, regions, near, zeros_ref, idx_ref, active_ref, count_ref, zone_ref, block_ref, own_ref, weight_ref):
    slots, _, lines = idx_ref.shape
    pieces = lines // LANES
    numbers = jnp.where(active_ref[...] > 0, count_ref[...], 0).astype(F32)

    def idx_row(p, j):
        return idx_ref[p, :, pl.ds(j * LANES, LANES)].astype(F32)

    block_ref[pl.ds(block_ref.shape[0] - 8, 8), :] = zeros_ref[...]
    for p in range(slots):
        for j in range(pieces):
            block_ref[pl.ds(p * pieces + j, 1), :] = idx_row(p, j)
    block_ref[pl.ds(slots * pieces, 1), :] = jnp.full((1, LANES), zone_ref[0].astype(F32))
    block_ref[pl.ds(slots * pieces + 1, 1), pl.ds(0, slots)] = numbers
    weight_ref[...] = line_tables(
        areas, regions, slots, pieces, near, idx_row, lambda p: numbers[:, p : p + 1], own_ref, weight_ref.shape[0]
    )


def first_kernel(slots, pieces, k_ref, load_ref, cap_ref, block_ref, edge_ref, *refs):
    *lean_refs, rest_ref, v_ref, lin_ref, kh_ref, kl_ref, over_ref = refs
    scens = lin_ref.shape[0]
    edge_ref[pl.ds(scens, block_ref.shape[0]), :] = block_ref[...]
    for ref, p in zip(lean_refs, (2, 4)):
        ref[pl.ds(scens, 2 * pieces), :] = block_ref[pl.ds(p * pieces, 2 * pieces), :]
        rest = ref.shape[0] - scens - 2 * pieces
        ref[pl.ds(scens + 2 * pieces, rest), :] = jnp.broadcast_to(
            block_ref[pl.ds(slots * pieces, 1), :], (rest, LANES)
        )
    high, low = halves(k_ref[0].T)
    kh_ref[...] = high
    kl_ref[...] = low
    lin_ref[...] = load_ref[0].T
    limits = cap_ref[...]

    def start(rows):
        return lin_ref[rows, :], jnp.zeros((CHAIN_ROWS, lin_ref.shape[1]), F32)

    def finish(rows, x, over):
        for ref in (edge_ref, *lean_refs):
            ref[rows, :] = x[:, :BOUNDARY]
        rest_ref[rows, :] = x[:, BOUNDARY:]
        v_ref[rows, :] = x + over

    run_sweeps(start, finish, lin_ref, over_ref, limits, kh_ref, kl_ref, INNER)


def share_kernel(areas, regions, near, zone_at, weight_ref, edge_ref, rest_ref, share_ref, *across_refs):
    scens = rest_ref.shape[0]
    x = jnp.concatenate([edge_ref[pl.ds(0, scens), :], rest_ref[...]], axis=1)
    sums = weighted_sums(weight_ref[...], x)
    if near:
        share_ref[...] = folded(sums[0:8, :])
        row_id = lax.broadcasted_iota(jnp.int32, (8, scens), 0)
        across = jnp.where(row_id == lax.axis_index("area"), sums[areas + 1 : areas + 2, :], 0.0)
        across_refs[0][...] = folded(jnp.where(row_id == areas, sums[areas : areas + 1, :], across))
        return
    if zone_at is not None:
        me = lax.axis_index("area") * regions + lax.axis_index("region")
        zone = edge_ref[pl.ds(zone_at, 1), pl.ds(0, 1)]
        row_id = lax.broadcasted_iota(jnp.int32, sums.shape, 0)
        sums = sums + jnp.where(row_id == areas * regions + 1 + me, zone, 0.0)
    share_ref[...] = sums[0 : share_ref.shape[0], :]


def append_kernel(scens, kept, zone_at, share_ref, across_ref, edge_ref, side_ref, pair_ref, full_ref, side_out_ref):
    pair = share_ref[...] + across_ref[...]
    rows = pair.shape[0]
    pair_ref[...] = pair
    full_ref[pl.ds(0, scens), :] = edge_ref[pl.ds(0, scens), :]
    full_ref[pl.ds(scens, rows), :] = pair
    if kept:
        full_ref[pl.ds(scens + rows, kept), :] = edge_ref[pl.ds(scens, kept), :]
        full_ref[pl.ds(scens + rows + kept, 1), :] = edge_ref[pl.ds(zone_at, 1), :]
    side_out_ref[...] = side_ref[...]


def live_lines(edge_ref, scens, slots, pieces, p):
    return edge_ref[pl.ds(scens + slots * pieces + 1, 1), pl.ds(p, 1)]


def by_area(values):
    me = lax.axis_index("area")
    out = []
    for k in range(4):
        mask = jnp.bitwise_xor(me, k)
        low = jnp.where(jnp.bitwise_and(mask, 1) == 0, values[0], values[1])
        high = jnp.where(jnp.bitwise_and(mask, 1) == 0, values[2], values[3])
        out.append(jnp.where(mask < 2, low, high))
    return out


def near_sums(scens, pair_ref, opposite_ref, far_ref, close_ref):
    rows = pl.ds(scens, pair_ref.shape[0])
    return unfolded((pair_ref[...] + close_ref[rows, :]) + (opposite_ref[...] + far_ref[rows, :]))


def near_prices(sums, zones, zone):
    price = sums[4:5, :] * SYSTEM_GAIN
    for k in range(4):
        price = price + jnp.where(zones[k] == zone, ZONE_GAIN, 0.0) * sums[k : k + 1, :]
    return price


def prices(shares, zones, total, regions, zone):
    ids = lax.broadcasted_iota(jnp.int32, zones.shape, 0)
    in_region = lax.rem(ids, regions) == lax.axis_index("region")
    gain = jnp.where(in_region & (zones == zone), ZONE_GAIN, 0.0) + SYSTEM_GAIN
    return jnp.sum(gain * shares[0:total, :], axis=0, keepdims=True)


class Mask(int):
    pass


class Plan:
    def __init__(self, areas, regions, scens, slots, pieces):
        self.near = (areas, regions) == (4, 2)
        self.scens, self.pieces = scens, pieces
        self.fold = 8 * (scens // LANES)
        if self.near:
            self.sources = [("area", Mask(2)), ("area", Mask(3)), ("area", Mask(1)), ("region", 1)]
            self.slots_of = [(2, 3), ((1, 0),), ((0, 1),), (4, 5)]
            self.buffer_of = [(2, 1), (1, 2), 0, 0, 3, 3]
            self.arrivals = [(0,), (1, 2, 3)]
            self.last = (1, 2, 3)
            return
        self.sources, self.slots_of, self.buffer_of = [], [], [None] * slots
        for p in (2, 3, 0, 1, 4, 5):
            axis, move, _ = SLOTS[p]
            source = (axis, move % (areas if axis == "area" else regions))
            if source not in self.sources:
                self.sources.append(source)
                self.slots_of.append(())
            self.buffer_of[p] = self.sources.index(source)
            self.slots_of[self.buffer_of[p]] += (p,)
        self.arrivals = [tuple(range(len(self.sources)))]
        self.last = self.arrivals[0]

    def line_row(self, b, p, j):
        back = SLOTS[p][2]
        if self.near:
            back -= {0: 2, 3: 4}.get(b, 0)
        return self.scens + (self.fold if self.near and b in (1, 2) else 0) + back * self.pieces + j

    def zone_row(self, b):
        return self.scens + (self.fold if b in (1, 2) else 0) + 2 * self.pieces


def choice(entry, read):
    if isinstance(entry, int):
        return read(entry)
    even = lax.rem(lax.axis_index("area"), 2) == 0
    return jnp.where(even, read(entry[0]), read(entry[1]))


def coupling_kernel(plan, held, own_ref, *refs):
    got, before, coupling_ref = refs[: len(held)], refs[len(held) : -1], refs[-1]
    lines = plan.pieces * LANES
    bus_id = lax.broadcasted_iota(jnp.int32, (BOUNDARY, LANES), 0).astype(F32)
    counts = []
    for b, g in zip(held, got):
        met = None
        for entry in plan.slots_of[b]:
            mine = choice(entry, lambda p: own_ref[:, pl.ds(p * lines, lines)])
            there = []
            for j in range(plan.pieces):
                row = choice(entry, lambda p: g[pl.ds(plan.line_row(b, p, j), 1), :])
                there.append(jnp.where(bus_id == row, 1.0, 0.0).astype(BF16))
            pairs = dot_nt(mine, jnp.concatenate(there, axis=1))
            met = pairs if met is None else met + pairs
        counts.append(met)
    counts_high, counts_low = halves(jnp.concatenate(counts, axis=1))
    high, low = halves(jnp.concatenate([g[pl.ds(0, plan.scens), :] for g in got], axis=1))
    out = dot_nt(high, counts_high) + dot_nt(low, counts_high) + dot_nt(high, counts_low)
    for ref in before:
        out = out + ref[...]
    coupling_ref[...] = out


def second_kernel(
    areas, regions, plan, zone_at, *refs
):
    *front, lin_ref, coupling_ref, v_ref, kh_ref, kl_ref, cap_ref, edge1_ref = refs[:-6]
    refs = (*front, *refs[-6:])
    edge_ref, rest_ref, sums_ref, lin2_ref, over_ref = refs[-5:]
    scens = lin_ref.shape[0]
    zone = edge1_ref[pl.ds(zone_at, 1), pl.ds(0, 1)]
    if plan.near:
        pair_ref, opposite_ref, *got = refs[:-6]
        sums = near_sums(scens, pair_ref, opposite_ref, got[1], got[2])
        zones = by_area([zone] + [got[b][pl.ds(plan.zone_row(b), 1), pl.ds(0, 1)] for b in (2, 0, 1)])
        price = near_prices(sums, zones, zone)
        sums_ref[pl.ds(0, 8), :] = sums
        sums_ref[pl.ds(8, 8), :] = jnp.zeros((8, scens), F32)
        for k in range(4):
            sums_ref[pl.ds(8 + k, 1), :] = jnp.broadcast_to(zones[k], (1, scens))
    else:
        total = areas * regions
        sums = refs[0][...]
        sums_ref[...] = sums
        price = prices(sums, sums[total + 1 : 2 * total + 1, :], total, regions, zone)
    price = jnp.broadcast_to(price, (8, scens)).T[:, 0:1]
    lin2_ref[:, pl.ds(0, BOUNDARY)] = lin_ref[:, pl.ds(0, BOUNDARY)] - price - coupling_ref[...]
    lin2_ref[:, pl.ds(BOUNDARY, BOUNDARY)] = lin_ref[:, pl.ds(BOUNDARY, BOUNDARY)] - price
    limits = cap_ref[...]

    def start(rows):
        clipped, over = clipping(v_ref[rows, :], limits)
        return lin2_ref[rows, :] + (clipped - over), over

    def finish(rows, x, over):
        edge_ref[rows, :] = x[:, :BOUNDARY]
        rest_ref[rows, :] = x[:, BOUNDARY:]

    run_sweeps(start, finish, lin2_ref, over_ref, limits, kh_ref, kl_ref, INNER)


def injection_kernel(edge_ref, rest_ref, injection_ref):
    scens = rest_ref.shape[0]
    injection_ref[0, pl.ds(0, BOUNDARY), :] = edge_ref[pl.ds(0, scens), :].T
    injection_ref[0, pl.ds(BOUNDARY, BOUNDARY), :] = rest_ref[...].T


def own_table_kernel(plan, own_ref, table_ref):
    pieces, scens = plan.pieces, plan.scens
    mine = own_ref[pl.ds(scens, own_ref.shape[0] - scens), :].T
    fill_table(plan, own_ref, table_ref, 0.5, lambda p, j: mine[:, p * pieces + j : p * pieces + j + 1])


def fill_table(plan, own_ref, table_ref, half, column):
    slots, pieces, scens = table_ref.shape[0], plan.pieces, plan.scens
    bus_id = lax.broadcasted_iota(jnp.int32, (LANES, BOUNDARY), 1).astype(F32)
    line_id = lax.broadcasted_iota(jnp.int32, (LANES, BOUNDARY), 0).astype(F32)
    for p in range(slots):
        number = live_lines(own_ref, scens, slots, pieces, p)
        for j in range(pieces):
            live = jnp.where(line_id + float(j * LANES) < number, half * SIGNS[p], 0.0)
            table_ref[p, pl.ds(j * LANES, LANES), :] = jnp.where(bus_id == column(p, j), live, 0.0).astype(BF16)


def table_kernel(plan, own_ref, *refs):
    got = refs[:-1]
    table_ref = refs[-1]
    slots, pieces = table_ref.shape[0], plan.pieces
    rows = []
    for p in range(slots):
        rows += [choice(plan.buffer_of[p], lambda b: got[b][pl.ds(plan.line_row(b, p, j), 1), :]) for j in range(pieces)]
        rows.append(jnp.zeros((8 - pieces, LANES), F32))
    theirs = jnp.concatenate(rows, axis=0).T
    fill_table(plan, own_ref, table_ref, -0.5, lambda p, j: theirs[:, p * 8 + j : p * 8 + j + 1])


def twice(x):
    return jnp.concatenate([x, x], axis=1)


def own_kernel(table_ref, edge_ref, flow_ref):
    scens = flow_ref.shape[2]
    parts = jnp.concatenate(halves(edge_ref[pl.ds(0, scens), :]), axis=1)
    for p in range(table_ref.shape[0]):
        flow_ref[p] = dot_nt(twice(table_ref[p]), parts)


def write_flows(plan, held, parts, table_ref, own_ref, flow_ref, flow_hbm, sems):
    copies = []
    for i, p in enumerate(held):
        part = choice(plan.buffer_of[p], lambda b: parts[b])
        flow_ref[i] = own_ref[p] + dot_nt(twice(table_ref[p]), part)
        copies.append(pltpu.make_async_copy(flow_ref.at[i], flow_hbm.at[0, p], sems.at[i]))
        copies[-1].start()
    return copies


def parts_of(plan, refs, held):
    return {b: jnp.concatenate(halves(ref[pl.ds(0, plan.scens), :]), axis=1) for b, ref in zip(held, refs)}


def parts_kernel(ref, part_ref):
    part_ref[...] = jnp.concatenate(halves(ref[pl.ds(0, part_ref.shape[0]), :]), axis=1)


def final_kernel(plan, table_ref, own_ref, *refs):
    *got, flow_hbm, done_ref, flow_ref, sems = refs
    if plan.near:
        parts = {0: got[0][...]}
        got = got[1:]
    else:
        parts = {}
    parts.update(parts_of(plan, got, plan.last))
    copies = write_flows(plan, (2, 3, 4, 5, 0, 1), parts, table_ref, own_ref, flow_ref, flow_hbm, sems)
    done_ref[...] = jnp.zeros(done_ref.shape, F32)
    for copy in copies:
        copy.wait()


def price_kernel(areas, regions, near, first_ref, done_ref, *refs):
    *rest, price_ref = refs
    if near:
        own, two, one, three = rest
        sums = first_ref[pl.ds(0, 8), :] + unfolded((own[...] + one[...]) + (two[...] + three[...]))
        zones = [first_ref[pl.ds(8 + k, 1), :] for k in range(4)]
        for z in range(ZONES):
            price_ref[pl.ds(z, 1), :] = near_prices(sums, zones, float(z))
        return
    total = areas * regions
    first = first_ref[...]
    zones = first[total + 1 : 2 * total + 1, :]
    for z in range(ZONES):
        price_ref[pl.ds(z, 1), :] = prices(first + rest[0][...], zones, total, regions, float(z))


def moved(x, axis, by):
    length = lax.axis_size(axis)
    if isinstance(by, Mask):
        return lax.ppermute(x, axis, [(i, i ^ by) for i in range(length)])
    return lax.ppermute(x, axis, [((i + by) % length, i) for i in range(length)])


def body(kkt_inverse, scen_load, capacity, pair_active, tie_counts, line_index, area_zone):
    areas = lax.axis_size("area")
    regions = lax.axis_size("region")
    total = areas * regions
    _, buses, scens = scen_load.shape
    _, slots, lines = line_index.shape
    rest = buses - BOUNDARY
    pieces = lines // LANES
    plan = Plan(areas, regions, scens, slots, pieces)
    near = plan.near
    zone_at = scens + slots * pieces
    share_rows = -(-(2 * total + 1) // 8) * 8
    weight_rows = 16 if near else -(-share_rows // 16) * 16

    def f32(*shape):
        return jax.ShapeDtypeStruct(shape, F32)

    def bf16(*shape):
        return jax.ShapeDtypeStruct(shape, BF16)

    def cost(flops):
        return pl.CostEstimate(flops=flops, bytes_accessed=0, transcendentals=0)

    def call(kernel, name, out_shape, operands, estimate=None, **more):
        return pl.pallas_call(
            kernel,
            out_shape=out_shape,
            in_specs=more.pop("in_specs", [VMEM] * len(operands)),
            out_specs=more.pop("out_specs", jax.tree.map(lambda _: VMEM, out_shape)),
            compiler_params=PARAMS,
            cost_estimate=estimate and cost(estimate),
            name=name,
            **more,
        )(*operands)

    def exchange_last(edge, rest, weights):
        got = [moved(edge, axis, move) for axis, move in plan.sources[::-1]][::-1]
        share, across = call(
            functools.partial(share_kernel, areas, regions, near, None),
            "mismatch_shares",
            [f32(plan.fold, LANES)] * 2,
            [weights, edge, rest],
        )
        pair = share + moved(across, "region", 1)
        return got, [pair, *(moved(pair, "area", Mask(mask)) for mask in (2, 1, 3))]

    def exchange(edge, rest, leans, weights, kept):
        held = edge.shape[0] > scens
        shapes = [f32(plan.fold, LANES)] * 2 if near else [f32(share_rows, scens)]
        share, *across = call(
            functools.partial(share_kernel, areas, regions, near, zone_at if held else None),
            "mismatch_shares",
            shapes,
            [weights, edge, rest],
        )
        if not near:
            return [moved(edge, axis, move) for axis, move in plan.sources], [lax.psum(share, ("area", "region"))]
        far, side = leans
        pair, full, side = call(
            functools.partial(append_kernel, scens, kept, zone_at),
            "pair_shares",
            [
                f32(plan.fold, LANES),
                f32(scens + plan.fold + -(-(kept and kept + 1) // 8) * 8, BOUNDARY),
                f32(*side.shape),
            ],
            [share, moved(across[0], "region", 1), edge, side],
        )
        got_side = moved(side, "region", 1)
        opposite = moved(pair, "area", Mask(2))
        got_near = moved(full, "area", Mask(1))
        got_other = moved(full, "area", Mask(3))
        return [moved(far, "area", Mask(2)), got_other, got_near, got_side], [pair, opposite]

    zeros = call(opening_kernel, "opening", f32(8, LANES), [], OPENING)
    lean_rows = -(-(scens + 2 * pieces + 1) // 8) * 8
    leans = [f32(lean_rows, BOUNDARY)] * 2 if near else []
    block, own, weights = call(
        functools.partial(lines_kernel, areas, regions, near),
        "line_blocks",
        [
            f32(-(-(slots * pieces + 2) // 8) * 8, LANES),
            bf16(BOUNDARY, slots * lines),
            f32(weight_rows, buses),
        ],
        [zeros, line_index.reshape(slots, 1, lines), pair_active, tie_counts, area_zone],
        in_specs=[VMEM] * 4 + [SMEM],
    )
    edge1, *more = call(
        functools.partial(first_kernel, slots, pieces),
        "first_round",
        [
            f32(scens + block.shape[0], BOUNDARY),
            *leans,
            f32(scens, rest),
            f32(scens, buses),
            f32(scens, buses),
            bf16(buses, buses),
            bf16(buses, buses),
        ],
        [kkt_inverse, scen_load, capacity, block],
        scratch_shapes=[pltpu.VMEM((scens, buses), F32)],
    )
    leans1, (rest1, state, lin, kh, kl) = more[: len(leans)], more[len(leans) :]
    got1, sums1 = exchange(edge1, rest1, leans1, weights, 2 * pieces)
    coupling = []
    for held in plan.arrivals:
        coupling = [
            call(
                functools.partial(coupling_kernel, plan, held),
                "coupling",
                f32(scens, BOUNDARY),
                [own, *(got1[b] for b in held), *coupling],
                BIG,
            )
        ]
    mine = call(functools.partial(own_table_kernel, plan), "own_table", bf16(slots, lines, BOUNDARY), [edge1])
    edge2, rest2, first = call(
        functools.partial(second_kernel, areas, regions, plan, zone_at),
        "second_round",
        [f32(scens, BOUNDARY), f32(scens, rest), f32(16 if near else share_rows, scens)],
        [*sums1, *(got1 if near else []), lin, *coupling, state, kh, kl, capacity, edge1, mine],
        scratch_shapes=[pltpu.VMEM((scens, buses), F32)] * 2,
    )
    if near:
        got2, sums2 = exchange_last(edge2, rest2, weights)
    else:
        got2, sums2 = exchange(edge2, rest2, [], weights, 0)
    injection = call(injection_kernel, "injection", f32(1, buses, scens), [edge2, rest2])
    theirs = call(functools.partial(table_kernel, plan), "line_table", bf16(slots, lines, BOUNDARY), [edge1, *got1])
    own_flow = call(own_kernel, "own_flows", f32(slots, lines, scens), [mine, edge2])
    operands = got2
    if near:
        far = call(parts_kernel, "injection_parts", bf16(scens, 2 * BOUNDARY), got2[:1], BIG)
        operands = [far, *(got2[b] for b in plan.last)]
    flow, done = call(
        functools.partial(final_kernel, plan),
        "tie_flows",
        (f32(1, slots, lines, scens), f32(8, LANES)),
        [theirs, own_flow, *operands],
        BIG,
        out_specs=(HBM, VMEM),
        scratch_shapes=[pltpu.VMEM((slots, lines, scens), F32), pltpu.SemaphoreType.DMA((slots,))],
    )
    price = call(
        functools.partial(price_kernel, areas, regions, near),
        "zone_prices",
        f32(ZONES, scens),
        [first, done, *sums2],
    )
    return injection, flow, price


def solution(mesh):
    placed = (
        P(("area", "region"), None, None),
        P(("area", "region"), None, ("group", "scen")),
        P(("area", "region"), None),
        P(("area", "region"), None),
        P(("area", "region"), None),
        P(("area", "region"), None, None),
        P(("area", "region")),
    )
    return jax.shard_map(
        body,
        mesh=mesh,
        in_specs=placed,
        out_specs=(
            P(("area", "region"), None, ("group", "scen")),
            P(("area", "region"), None, None, ("group", "scen")),
            P("region", ("group", "scen")),
        ),
        check_vma=False,
    )
```

```python
import functools

import jax
import jax.numpy as jnp
from jax import lax
from jax.experimental import pallas as pl
from jax.experimental.pallas import tpu as pltpu
from jax.sharding import PartitionSpec as P

ZONES = 4
INNER = 24
BOUNDARY = 128
LANES = 128
ZONE_GAIN = 0.004
SYSTEM_GAIN = 0.001
SLOTS = (
    ("area", 1, 1),
    ("area", -1, 0),
    ("area", 2, 3),
    ("area", -2, 2),
    ("region", 1, 5),
    ("region", -1, 4),
)
SIGNS = (1.0, -1.0, 1.0, -1.0, 1.0, -1.0)
CHAIN_ROWS = 32
UNROLL = 4
BIG = 4 * 10**9
OPENING = 10**11

F32 = jnp.float32
BF16 = jnp.bfloat16
VMEM = pl.BlockSpec(memory_space=pltpu.VMEM)
SMEM = pl.BlockSpec(memory_space=pltpu.SMEM)
HBM = pl.BlockSpec(memory_space=pltpu.HBM)
PARAMS = pltpu.CompilerParams(vmem_limit_bytes=40 * 2**20)


def dot(a, b):
    return jnp.dot(a, b, preferred_element_type=F32)


def dot_nt(a, b):
    return lax.dot_general(a, b, (((1,), (1,)), ((), ())), preferred_element_type=F32)


def halves(x):
    high = x.astype(BF16)
    return high, (x - high.astype(F32)).astype(BF16)


def thirds(x):
    high = x.astype(BF16)
    rest = x - high.astype(F32)
    middle = rest.astype(BF16)
    return high, middle, (rest - middle.astype(F32)).astype(BF16)


def clipping(v, limits):
    clipped = jnp.clip(v, -limits, limits)
    return clipped, v - clipped


def run_sweeps(start, finish, lin_ref, over_ref, limits, kh_ref, kl_ref, count):
    scens, buses = lin_ref.shape
    chains = scens // CHAIN_ROWS

    def scoped(*accumulators):
        highs, lows = accumulators[:chains], accumulators[chains:]
        pltpu.matmul_push_rhs(kh_ref[...], 0, 0)
        pltpu.matmul_push_rhs(kl_ref[...], 0, 1)

        def issue(i, x, load=None):
            high, low = halves(x)
            pltpu.matmul_acc_lhs(highs[i], high, load)
            pltpu.matmul_acc_lhs(highs[i], low)
            pltpu.matmul_acc_lhs(lows[i], high, load)

        def rows_of(i):
            return pl.ds(i * CHAIN_ROWS, CHAIN_ROWS)

        def taken(i):
            return pltpu.matmul_pop(highs[i]) + pltpu.matmul_pop(lows[i])

        for i in range(chains):
            x, over = start(rows_of(i))
            over_ref[rows_of(i), :] = over
            issue(i, x, 0 if i == 0 else None)

        def sweep(_, carry):
            for i in range(chains):
                rows = rows_of(i)
                clipped, over = clipping(taken(i) + over_ref[rows, :], limits)
                over_ref[rows, :] = over
                issue(i, lin_ref[rows, :] + (clipped - over))
            return carry

        lax.fori_loop(0, count - 1, sweep, 0, unroll=UNROLL)
        for i in range(chains):
            finish(rows_of(i), taken(i), over_ref[rows_of(i), :])

    pl.run_scoped(
        scoped,
        *[pltpu.ACC(0)((CHAIN_ROWS, buses), F32)] * chains,
        *[pltpu.ACC(1)((CHAIN_ROWS, buses), F32)] * chains,
    )


def line_tables(areas, regions, slots, pieces, near, idx_row, number, own_ref, rows):
    me_area, me_region = lax.axis_index("area"), lax.axis_index("region")
    here = me_area if near else me_area * regions + me_region
    width = -(-rows // LANES) * LANES
    row_id = lax.broadcasted_iota(jnp.int32, (1, width), 1)
    line_id = lax.broadcasted_iota(jnp.int32, (1, LANES), 1).astype(F32)
    bus_id = lax.broadcasted_iota(jnp.int32, (BOUNDARY, LANES), 0).astype(F32)
    weights = jnp.zeros((BOUNDARY, width), F32)
    for p in range(slots):
        axis, move, _ = SLOTS[p]
        if axis == "area":
            other = lax.rem(me_area + move % areas, areas)
            there = other if near else other * regions + me_region
        else:
            there = areas + 1 if near else me_area * regions + lax.rem(me_region + move % regions, regions)
        coefficient = jnp.where(row_id == there, 0.5, 0.0) - jnp.where(row_id == here, 0.5, 0.0)
        met = None
        for j in range(pieces):
            row = jnp.where(line_id + float(j * LANES) < number(p), idx_row(p, j), -1.0)
            onehot = jnp.where(bus_id == row, 1.0, 0.0)
            own_ref[:, pl.ds((p * pieces + j) * LANES, LANES)] = onehot.astype(BF16)
            met = onehot if met is None else met + onehot
        weights = weights + jnp.sum(met, axis=1, keepdims=True) * coefficient
    last = areas if near else areas * regions
    mine = jnp.where((row_id == here) | (row_id == last), 1.0, 0.0)
    weights = jnp.concatenate([weights + mine, jnp.broadcast_to(mine, (BOUNDARY, width))], axis=0)
    return weights.T[0:rows, :]


def weighted_sums(weights, x):
    wh, wl = halves(weights)
    xh, xm, xl = thirds(x)
    return dot_nt(wh, xh) + (dot_nt(wh, xm) + dot_nt(wl, xh)) + (dot_nt(wh, xl) + dot_nt(wl, xm))


def folded(x):
    return jnp.concatenate([x[:, j : j + LANES] for j in range(0, x.shape[1], LANES)], axis=0)


def unfolded(x):
    return jnp.concatenate([x[j : j + 8, :] for j in range(0, x.shape[0], 8)], axis=1)


def opening_kernel(zeros_ref):
    zeros_ref[...] = jnp.zeros(zeros_ref.shape, F32)


def lines_kernel(areas, regions, near, zeros_ref, idx_ref, active_ref, count_ref, zone_ref, block_ref, own_ref, weight_ref):
    slots, _, lines = idx_ref.shape
    pieces = lines // LANES
    numbers = jnp.where(active_ref[...] > 0, count_ref[...], 0).astype(F32)

    def idx_row(p, j):
        return idx_ref[p, :, pl.ds(j * LANES, LANES)].astype(F32)

    block_ref[pl.ds(block_ref.shape[0] - 8, 8), :] = zeros_ref[...]
    for p in range(slots):
        for j in range(pieces):
            block_ref[pl.ds(p * pieces + j, 1), :] = idx_row(p, j)
    block_ref[pl.ds(slots * pieces, 1), :] = jnp.full((1, LANES), zone_ref[0].astype(F32))
    block_ref[pl.ds(slots * pieces + 1, 1), pl.ds(0, slots)] = numbers
    weight_ref[...] = line_tables(
        areas, regions, slots, pieces, near, idx_row, lambda p: numbers[:, p : p + 1], own_ref, weight_ref.shape[0]
    )


def first_kernel(slots, pieces, k_ref, load_ref, cap_ref, block_ref, edge_ref, *refs):
    *lean_refs, rest_ref, v_ref, lin_ref, kh_ref, kl_ref, over_ref = refs
    scens = lin_ref.shape[0]
    edge_ref[pl.ds(scens, block_ref.shape[0]), :] = block_ref[...]
    for ref, p in zip(lean_refs, (2, 4)):
        ref[pl.ds(scens, 2 * pieces), :] = block_ref[pl.ds(p * pieces, 2 * pieces), :]
        rest = ref.shape[0] - scens - 2 * pieces
        ref[pl.ds(scens + 2 * pieces, rest), :] = jnp.broadcast_to(
            block_ref[pl.ds(slots * pieces, 1), :], (rest, LANES)
        )
    high, low = halves(k_ref[0].T)
    kh_ref[...] = high
    kl_ref[...] = low
    lin_ref[...] = load_ref[0].T
    limits = cap_ref[...]

    def start(rows):
        return lin_ref[rows, :], jnp.zeros((CHAIN_ROWS, lin_ref.shape[1]), F32)

    def finish(rows, x, over):
        for ref in (edge_ref, *lean_refs):
            ref[rows, :] = x[:, :BOUNDARY]
        rest_ref[rows, :] = x[:, BOUNDARY:]
        v_ref[rows, :] = x + over

    run_sweeps(start, finish, lin_ref, over_ref, limits, kh_ref, kl_ref, INNER)


def share_kernel(areas, regions, near, zone_at, weight_ref, edge_ref, rest_ref, share_ref, *across_refs):
    scens = rest_ref.shape[0]
    x = jnp.concatenate([edge_ref[pl.ds(0, scens), :], rest_ref[...]], axis=1)
    sums = weighted_sums(weight_ref[...], x)
    if near:
        share_ref[...] = folded(sums[0:8, :])
        row_id = lax.broadcasted_iota(jnp.int32, (8, scens), 0)
        across = jnp.where(row_id == lax.axis_index("area"), sums[areas + 1 : areas + 2, :], 0.0)
        across_refs[0][...] = folded(jnp.where(row_id == areas, sums[areas : areas + 1, :], across))
        return
    if zone_at is not None:
        me = lax.axis_index("area") * regions + lax.axis_index("region")
        zone = edge_ref[pl.ds(zone_at, 1), pl.ds(0, 1)]
        row_id = lax.broadcasted_iota(jnp.int32, sums.shape, 0)
        sums = sums + jnp.where(row_id == areas * regions + 1 + me, zone, 0.0)
    share_ref[...] = sums[0 : share_ref.shape[0], :]


def append_kernel(scens, kept, zone_at, share_ref, across_ref, edge_ref, side_ref, pair_ref, full_ref, side_out_ref):
    pair = share_ref[...] + across_ref[...]
    rows = pair.shape[0]
    pair_ref[...] = pair
    full_ref[pl.ds(0, scens), :] = edge_ref[pl.ds(0, scens), :]
    full_ref[pl.ds(scens, rows), :] = pair
    if kept:
        full_ref[pl.ds(scens + rows, kept), :] = edge_ref[pl.ds(scens, kept), :]
        full_ref[pl.ds(scens + rows + kept, 1), :] = edge_ref[pl.ds(zone_at, 1), :]
    side_out_ref[...] = side_ref[...]


def live_lines(edge_ref, scens, slots, pieces, p):
    return edge_ref[pl.ds(scens + slots * pieces + 1, 1), pl.ds(p, 1)]


def by_area(values):
    me = lax.axis_index("area")
    out = []
    for k in range(4):
        mask = jnp.bitwise_xor(me, k)
        low = jnp.where(jnp.bitwise_and(mask, 1) == 0, values[0], values[1])
        high = jnp.where(jnp.bitwise_and(mask, 1) == 0, values[2], values[3])
        out.append(jnp.where(mask < 2, low, high))
    return out


def near_sums(scens, pair_ref, opposite_ref, far_ref, close_ref):
    rows = pl.ds(scens, pair_ref.shape[0])
    return unfolded((pair_ref[...] + close_ref[rows, :]) + (opposite_ref[...] + far_ref[rows, :]))


def near_prices(sums, zones, zone):
    price = sums[4:5, :] * SYSTEM_GAIN
    for k in range(4):
        price = price + jnp.where(zones[k] == zone, ZONE_GAIN, 0.0) * sums[k : k + 1, :]
    return price


def prices(shares, zones, total, regions, zone):
    ids = lax.broadcasted_iota(jnp.int32, zones.shape, 0)
    in_region = lax.rem(ids, regions) == lax.axis_index("region")
    gain = jnp.where(in_region & (zones == zone), ZONE_GAIN, 0.0) + SYSTEM_GAIN
    return jnp.sum(gain * shares[0:total, :], axis=0, keepdims=True)


class Mask(int):
    pass


class Plan:
    def __init__(self, areas, regions, scens, slots, pieces):
        self.near = (areas, regions) == (4, 2)
        self.scens, self.pieces = scens, pieces
        self.fold = 8 * (scens // LANES)
        if self.near:
            self.sources = [("area", Mask(2)), ("area", Mask(3)), ("area", Mask(1)), ("region", 1)]
            self.slots_of = [(2, 3), ((1, 0),), ((0, 1),), (4, 5)]
            self.buffer_of = [(2, 1), (1, 2), 0, 0, 3, 3]
            self.arrivals = [(0,), (3,), (1, 2)]
            self.last = (1, 2, 3)
            return
        self.sources, self.slots_of, self.buffer_of = [], [], [None] * slots
        for p in (2, 3, 0, 1, 4, 5):
            axis, move, _ = SLOTS[p]
            source = (axis, move % (areas if axis == "area" else regions))
            if source not in self.sources:
                self.sources.append(source)
                self.slots_of.append(())
            self.buffer_of[p] = self.sources.index(source)
            self.slots_of[self.buffer_of[p]] += (p,)
        self.arrivals = [tuple(range(len(self.sources)))]
        self.last = self.arrivals[0]

    def line_row(self, b, p, j):
        back = SLOTS[p][2]
        if self.near:
            back -= {0: 2, 3: 4}.get(b, 0)
        return self.scens + (self.fold if self.near and b in (1, 2) else 0) + back * self.pieces + j

    def zone_row(self, b):
        return self.scens + (self.fold if b in (1, 2) else 0) + 2 * self.pieces


def choice(entry, read):
    if isinstance(entry, int):
        return read(entry)
    even = lax.rem(lax.axis_index("area"), 2) == 0
    return jnp.where(even, read(entry[0]), read(entry[1]))


def coupling_kernel(plan, held, own_ref, *refs):
    got, before, coupling_ref = refs[: len(held)], refs[len(held) : -1], refs[-1]
    lines = plan.pieces * LANES
    bus_id = lax.broadcasted_iota(jnp.int32, (BOUNDARY, LANES), 0).astype(F32)
    counts = []
    for b, g in zip(held, got):
        met = None
        for entry in plan.slots_of[b]:
            mine = choice(entry, lambda p: own_ref[:, pl.ds(p * lines, lines)])
            there = []
            for j in range(plan.pieces):
                row = choice(entry, lambda p: g[pl.ds(plan.line_row(b, p, j), 1), :])
                there.append(jnp.where(bus_id == row, 1.0, 0.0).astype(BF16))
            pairs = dot_nt(mine, jnp.concatenate(there, axis=1))
            met = pairs if met is None else met + pairs
        counts.append(met)
    counts_high, counts_low = halves(jnp.concatenate(counts, axis=1))
    high, low = halves(jnp.concatenate([g[pl.ds(0, plan.scens), :] for g in got], axis=1))
    out = dot_nt(high, counts_high) + dot_nt(low, counts_high) + dot_nt(high, counts_low)
    for ref in before:
        out = out + ref[...]
    coupling_ref[...] = out


def second_kernel(
    areas, regions, plan, zone_at, *refs
):
    *front, lin_ref, coupling_ref, v_ref, kh_ref, kl_ref, cap_ref, edge1_ref = refs[:-6]
    refs = (*front, *refs[-6:])
    edge_ref, rest_ref, sums_ref, lin2_ref, over_ref = refs[-5:]
    scens = lin_ref.shape[0]
    zone = edge1_ref[pl.ds(zone_at, 1), pl.ds(0, 1)]
    if plan.near:
        pair_ref, opposite_ref, *got = refs[:-6]
        sums = near_sums(scens, pair_ref, opposite_ref, got[1], got[2])
        zones = by_area([zone] + [got[b][pl.ds(plan.zone_row(b), 1), pl.ds(0, 1)] for b in (2, 0, 1)])
        price = near_prices(sums, zones, zone)
        sums_ref[pl.ds(0, 8), :] = sums
        sums_ref[pl.ds(8, 8), :] = jnp.zeros((8, scens), F32)
        for k in range(4):
            sums_ref[pl.ds(8 + k, 1), :] = jnp.broadcast_to(zones[k], (1, scens))
    else:
        total = areas * regions
        sums = refs[0][...]
        sums_ref[...] = sums
        price = prices(sums, sums[total + 1 : 2 * total + 1, :], total, regions, zone)
    price_ref = over_ref
    price_ref[...] = jnp.broadcast_to(jnp.broadcast_to(price, (8, scens)).T[:, 0:1], price_ref.shape)
    limits = cap_ref[...]

    def start(rows):
        lin = lin_ref[rows, :] - price_ref[rows, :]
        lin = jnp.concatenate([lin[:, :BOUNDARY] - coupling_ref[rows, :], lin[:, BOUNDARY:]], axis=1)
        lin2_ref[rows, :] = lin
        clipped, over = clipping(v_ref[rows, :], limits)
        return lin + (clipped - over), over

    def finish(rows, x, over):
        edge_ref[rows, :] = x[:, :BOUNDARY]
        rest_ref[rows, :] = x[:, BOUNDARY:]

    run_sweeps(start, finish, lin2_ref, over_ref, limits, kh_ref, kl_ref, INNER)


def injection_kernel(edge_ref, rest_ref, injection_ref):
    scens = rest_ref.shape[0]
    injection_ref[0, pl.ds(0, BOUNDARY), :] = edge_ref[pl.ds(0, scens), :].T
    injection_ref[0, pl.ds(BOUNDARY, BOUNDARY), :] = rest_ref[...].T


def own_table_kernel(plan, own_ref, table_ref):
    pieces, scens = plan.pieces, plan.scens
    mine = own_ref[pl.ds(scens, own_ref.shape[0] - scens), :].T
    fill_table(plan, own_ref, table_ref, 0.5, lambda p, j: mine[:, p * pieces + j : p * pieces + j + 1])


def fill_table(plan, own_ref, table_ref, half, column):
    slots, pieces, scens = table_ref.shape[0], plan.pieces, plan.scens
    bus_id = lax.broadcasted_iota(jnp.int32, (LANES, BOUNDARY), 1).astype(F32)
    line_id = lax.broadcasted_iota(jnp.int32, (LANES, BOUNDARY), 0).astype(F32)
    for p in range(slots):
        number = live_lines(own_ref, scens, slots, pieces, p)
        for j in range(pieces):
            live = jnp.where(line_id + float(j * LANES) < number, half * SIGNS[p], 0.0)
            table_ref[p, pl.ds(j * LANES, LANES), :] = jnp.where(bus_id == column(p, j), live, 0.0).astype(BF16)


def table_kernel(plan, own_ref, *refs):
    got = refs[:-1]
    table_ref = refs[-1]
    slots, pieces = table_ref.shape[0], plan.pieces
    rows = []
    for p in range(slots):
        rows += [choice(plan.buffer_of[p], lambda b: got[b][pl.ds(plan.line_row(b, p, j), 1), :]) for j in range(pieces)]
        rows.append(jnp.zeros((8 - pieces, LANES), F32))
    theirs = jnp.concatenate(rows, axis=0).T
    fill_table(plan, own_ref, table_ref, -0.5, lambda p, j: theirs[:, p * 8 + j : p * 8 + j + 1])


def twice(x):
    return jnp.concatenate([x, x], axis=1)


def own_kernel(table_ref, edge_ref, flow_ref):
    scens = flow_ref.shape[2]
    parts = jnp.concatenate(halves(edge_ref[pl.ds(0, scens), :]), axis=1)
    for p in range(table_ref.shape[0]):
        flow_ref[p] = dot_nt(twice(table_ref[p]), parts)


def write_flows(plan, held, parts, table_ref, own_ref, flow_ref, flow_hbm, sems):
    copies = []
    for i, p in enumerate(held):
        part = choice(plan.buffer_of[p], lambda b: parts[b])
        flow_ref[i] = own_ref[p] + dot_nt(twice(table_ref[p]), part)
        copies.append(pltpu.make_async_copy(flow_ref.at[i], flow_hbm.at[0, p], sems.at[i]))
        copies[-1].start()
    return copies


def parts_of(plan, refs, held):
    return {b: jnp.concatenate(halves(ref[pl.ds(0, plan.scens), :]), axis=1) for b, ref in zip(held, refs)}


def parts_kernel(ref, part_ref):
    part_ref[...] = jnp.concatenate(halves(ref[pl.ds(0, part_ref.shape[0]), :]), axis=1)


def final_kernel(plan, table_ref, own_ref, *refs):
    *got, flow_hbm, done_ref, flow_ref, sems = refs
    if plan.near:
        parts = {0: got[0][...]}
        got = got[1:]
    else:
        parts = {}
    parts.update(parts_of(plan, got, plan.last))
    copies = write_flows(plan, (2, 3, 4, 5, 0, 1), parts, table_ref, own_ref, flow_ref, flow_hbm, sems)
    done_ref[...] = jnp.zeros(done_ref.shape, F32)
    for copy in copies:
        copy.wait()


def price_kernel(areas, regions, near, first_ref, done_ref, *refs):
    *rest, price_ref = refs
    if near:
        own, two, one, three = rest
        sums = first_ref[pl.ds(0, 8), :] + unfolded((own[...] + one[...]) + (two[...] + three[...]))
        zones = [first_ref[pl.ds(8 + k, 1), :] for k in range(4)]
        for z in range(ZONES):
            price_ref[pl.ds(z, 1), :] = near_prices(sums, zones, float(z))
        return
    total = areas * regions
    first = first_ref[...]
    zones = first[total + 1 : 2 * total + 1, :]
    for z in range(ZONES):
        price_ref[pl.ds(z, 1), :] = prices(first + rest[0][...], zones, total, regions, float(z))


def moved(x, axis, by):
    length = lax.axis_size(axis)
    if isinstance(by, Mask):
        return lax.ppermute(x, axis, [(i, i ^ by) for i in range(length)])
    return lax.ppermute(x, axis, [((i + by) % length, i) for i in range(length)])


def body(kkt_inverse, scen_load, capacity, pair_active, tie_counts, line_index, area_zone):
    areas = lax.axis_size("area")
    regions = lax.axis_size("region")
    total = areas * regions
    _, buses, scens = scen_load.shape
    _, slots, lines = line_index.shape
    rest = buses - BOUNDARY
    pieces = lines // LANES
    plan = Plan(areas, regions, scens, slots, pieces)
    near = plan.near
    zone_at = scens + slots * pieces
    share_rows = -(-(2 * total + 1) // 8) * 8
    weight_rows = 16 if near else -(-share_rows // 16) * 16

    def f32(*shape):
        return jax.ShapeDtypeStruct(shape, F32)

    def bf16(*shape):
        return jax.ShapeDtypeStruct(shape, BF16)

    def cost(flops):
        return pl.CostEstimate(flops=flops, bytes_accessed=0, transcendentals=0)

    def call(kernel, name, out_shape, operands, estimate=None, **more):
        return pl.pallas_call(
            kernel,
            out_shape=out_shape,
            in_specs=more.pop("in_specs", [VMEM] * len(operands)),
            out_specs=more.pop("out_specs", jax.tree.map(lambda _: VMEM, out_shape)),
            compiler_params=PARAMS,
            cost_estimate=estimate and cost(estimate),
            name=name,
            **more,
        )(*operands)

    def exchange_last(edge, rest, weights):
        got = [moved(edge, axis, move) for axis, move in plan.sources[::-1]][::-1]
        share, across = call(
            functools.partial(share_kernel, areas, regions, near, None),
            "mismatch_shares",
            [f32(plan.fold, LANES)] * 2,
            [weights, edge, rest],
        )
        pair = share + moved(across, "region", 1)
        return got, [pair, *(moved(pair, "area", Mask(mask)) for mask in (2, 1, 3))]

    def exchange(edge, rest, leans, weights, kept):
        held = edge.shape[0] > scens
        shapes = [f32(plan.fold, LANES)] * 2 if near else [f32(share_rows, scens)]
        share, *across = call(
            functools.partial(share_kernel, areas, regions, near, zone_at if held else None),
            "mismatch_shares",
            shapes,
            [weights, edge, rest],
        )
        if not near:
            return [moved(edge, axis, move) for axis, move in plan.sources], [lax.psum(share, ("area", "region"))]
        far, side = leans
        pair, full, side = call(
            functools.partial(append_kernel, scens, kept, zone_at),
            "pair_shares",
            [
                f32(plan.fold, LANES),
                f32(scens + plan.fold + -(-(kept and kept + 1) // 8) * 8, BOUNDARY),
                f32(*side.shape),
            ],
            [share, moved(across[0], "region", 1), edge, side],
        )
        got_side = moved(side, "region", 1)
        opposite = moved(pair, "area", Mask(2))
        got_near = moved(full, "area", Mask(1))
        got_other = moved(full, "area", Mask(3))
        return [moved(far, "area", Mask(2)), got_other, got_near, got_side], [pair, opposite]

    zeros = call(opening_kernel, "opening", f32(8, LANES), [], OPENING)
    lean_rows = -(-(scens + 2 * pieces + 1) // 8) * 8
    leans = [f32(lean_rows, BOUNDARY)] * 2 if near else []
    block, own, weights = call(
        functools.partial(lines_kernel, areas, regions, near),
        "line_blocks",
        [
            f32(-(-(slots * pieces + 2) // 8) * 8, LANES),
            bf16(BOUNDARY, slots * lines),
            f32(weight_rows, buses),
        ],
        [zeros, line_index.reshape(slots, 1, lines), pair_active, tie_counts, area_zone],
        in_specs=[VMEM] * 4 + [SMEM],
    )
    edge1, *more = call(
        functools.partial(first_kernel, slots, pieces),
        "first_round",
        [
            f32(scens + block.shape[0], BOUNDARY),
            *leans,
            f32(scens, rest),
            f32(scens, buses),
            f32(scens, buses),
            bf16(buses, buses),
            bf16(buses, buses),
        ],
        [kkt_inverse, scen_load, capacity, block],
        scratch_shapes=[pltpu.VMEM((scens, buses), F32)],
    )
    leans1, (rest1, state, lin, kh, kl) = more[: len(leans)], more[len(leans) :]
    got1, sums1 = exchange(edge1, rest1, leans1, weights, 2 * pieces)
    coupling = []
    for held in plan.arrivals:
        coupling = [
            call(
                functools.partial(coupling_kernel, plan, held),
                "coupling",
                f32(scens, BOUNDARY),
                [own, *(got1[b] for b in held), *coupling],
                BIG,
            )
        ]
    mine = call(functools.partial(own_table_kernel, plan), "own_table", bf16(slots, lines, BOUNDARY), [edge1])
    edge2, rest2, first = call(
        functools.partial(second_kernel, areas, regions, plan, zone_at),
        "second_round",
        [f32(scens, BOUNDARY), f32(scens, rest), f32(16 if near else share_rows, scens)],
        [*sums1, *(got1 if near else []), lin, *coupling, state, kh, kl, capacity, edge1, mine],
        scratch_shapes=[pltpu.VMEM((scens, buses), F32)] * 2,
    )
    if near:
        got2, sums2 = exchange_last(edge2, rest2, weights)
    else:
        got2, sums2 = exchange(edge2, rest2, [], weights, 0)
    injection = call(injection_kernel, "injection", f32(1, buses, scens), [edge2, rest2])
    theirs = call(functools.partial(table_kernel, plan), "line_table", bf16(slots, lines, BOUNDARY), [edge1, *got1])
    own_flow = call(own_kernel, "own_flows", f32(slots, lines, scens), [mine, edge2])
    operands = got2
    if near:
        far = call(parts_kernel, "injection_parts", bf16(scens, 2 * BOUNDARY), got2[:1], BIG)
        operands = [far, *(got2[b] for b in plan.last)]
    flow, done = call(
        functools.partial(final_kernel, plan),
        "tie_flows",
        (f32(1, slots, lines, scens), f32(8, LANES)),
        [theirs, own_flow, *operands],
        BIG,
        out_specs=(HBM, VMEM),
        scratch_shapes=[pltpu.VMEM((slots, lines, scens), F32), pltpu.SemaphoreType.DMA((slots,))],
    )
    price = call(
        functools.partial(price_kernel, areas, regions, near),
        "zone_prices",
        f32(ZONES, scens),
        [first, done, *sums2],
    )
    return injection, flow, price


def solution(mesh):
    placed = (
        P(("area", "region"), None, None),
        P(("area", "region"), None, ("group", "scen")),
        P(("area", "region"), None),
        P(("area", "region"), None),
        P(("area", "region"), None),
        P(("area", "region"), None, None),
        P(("area", "region")),
    )
    return jax.shard_map(
        body,
        mesh=mesh,
        in_specs=placed,
        out_specs=(
            P(("area", "region"), None, ("group", "scen")),
            P(("area", "region"), None, None, ("group", "scen")),
            P("region", ("group", "scen")),
        ),
        check_vma=False,
    )
```

```python
import functools

import jax
import jax.numpy as jnp
from jax import lax
from jax.experimental import pallas as pl
from jax.experimental.pallas import tpu as pltpu
from jax.sharding import PartitionSpec as P

ZONES = 4
INNER = 24
BOUNDARY = 128
LANES = 128
ZONE_GAIN = 0.004
SYSTEM_GAIN = 0.001
SLOTS = (
    ("area", 1, 1),
    ("area", -1, 0),
    ("area", 2, 3),
    ("area", -2, 2),
    ("region", 1, 5),
    ("region", -1, 4),
)
SIGNS = (1.0, -1.0, 1.0, -1.0, 1.0, -1.0)
CHAIN_ROWS = 32
UNROLL = 4
BIG = 4 * 10**9
OPENING = 10**11

F32 = jnp.float32
BF16 = jnp.bfloat16
VMEM = pl.BlockSpec(memory_space=pltpu.VMEM)
SMEM = pl.BlockSpec(memory_space=pltpu.SMEM)
HBM = pl.BlockSpec(memory_space=pltpu.HBM)
PARAMS = pltpu.CompilerParams(vmem_limit_bytes=40 * 2**20)


def dot(a, b):
    return jnp.dot(a, b, preferred_element_type=F32)


def dot_nt(a, b):
    return lax.dot_general(a, b, (((1,), (1,)), ((), ())), preferred_element_type=F32)


def halves(x):
    high = x.astype(BF16)
    return high, (x - high.astype(F32)).astype(BF16)


def thirds(x):
    high = x.astype(BF16)
    rest = x - high.astype(F32)
    middle = rest.astype(BF16)
    return high, middle, (rest - middle.astype(F32)).astype(BF16)


def clipping(v, limits):
    clipped = jnp.clip(v, -limits, limits)
    return clipped, v - clipped


def run_sweeps(start, finish, lin_ref, over_ref, limits, kh_ref, kl_ref, count):
    scens, buses = lin_ref.shape
    chains = scens // CHAIN_ROWS

    def scoped(*accumulators):
        highs, lows = accumulators[:chains], accumulators[chains:]
        pltpu.matmul_push_rhs(kh_ref[...], 0, 0)
        pltpu.matmul_push_rhs(kl_ref[...], 0, 1)

        def issue(i, x, load=None):
            high, low = halves(x)
            pltpu.matmul_acc_lhs(highs[i], high, load)
            pltpu.matmul_acc_lhs(highs[i], low)
            pltpu.matmul_acc_lhs(lows[i], high, load)

        def rows_of(i):
            return pl.ds(i * CHAIN_ROWS, CHAIN_ROWS)

        def taken(i):
            return pltpu.matmul_pop(highs[i]) + pltpu.matmul_pop(lows[i])

        for i in range(chains):
            x, over = start(rows_of(i))
            over_ref[rows_of(i), :] = over
            issue(i, x, 0 if i == 0 else None)

        def sweep(_, carry):
            for i in range(chains):
                rows = rows_of(i)
                clipped, over = clipping(taken(i) + over_ref[rows, :], limits)
                over_ref[rows, :] = over
                issue(i, lin_ref[rows, :] + (clipped - over))
            return carry

        lax.fori_loop(0, count - 1, sweep, 0, unroll=UNROLL)
        for i in range(chains):
            finish(rows_of(i), taken(i), over_ref[rows_of(i), :])

    pl.run_scoped(
        scoped,
        *[pltpu.ACC(0)((CHAIN_ROWS, buses), F32)] * chains,
        *[pltpu.ACC(1)((CHAIN_ROWS, buses), F32)] * chains,
    )


def line_tables(areas, regions, slots, pieces, near, idx_row, number, own_ref, rows):
    me_area, me_region = lax.axis_index("area"), lax.axis_index("region")
    here = me_area if near else me_area * regions + me_region
    width = -(-rows // LANES) * LANES
    row_id = lax.broadcasted_iota(jnp.int32, (1, width), 1)
    line_id = lax.broadcasted_iota(jnp.int32, (1, LANES), 1).astype(F32)
    bus_id = lax.broadcasted_iota(jnp.int32, (BOUNDARY, LANES), 0).astype(F32)
    weights = jnp.zeros((BOUNDARY, width), F32)
    for p in range(slots):
        axis, move, _ = SLOTS[p]
        if axis == "area":
            other = lax.rem(me_area + move % areas, areas)
            there = other if near else other * regions + me_region
        else:
            there = areas + 1 if near else me_area * regions + lax.rem(me_region + move % regions, regions)
        coefficient = jnp.where(row_id == there, 0.5, 0.0) - jnp.where(row_id == here, 0.5, 0.0)
        met = None
        for j in range(pieces):
            row = jnp.where(line_id + float(j * LANES) < number(p), idx_row(p, j), -1.0)
            onehot = jnp.where(bus_id == row, 1.0, 0.0)
            own_ref[:, pl.ds((p * pieces + j) * LANES, LANES)] = onehot.astype(BF16)
            met = onehot if met is None else met + onehot
        weights = weights + jnp.sum(met, axis=1, keepdims=True) * coefficient
    last = areas if near else areas * regions
    mine = jnp.where((row_id == here) | (row_id == last), 1.0, 0.0)
    weights = jnp.concatenate([weights + mine, jnp.broadcast_to(mine, (BOUNDARY, width))], axis=0)
    return weights.T[0:rows, :]


def weighted_sums(weights, x):
    wh, wl = halves(weights)
    xh, xm, xl = thirds(x)
    return dot_nt(wh, xh) + (dot_nt(wh, xm) + dot_nt(wl, xh)) + (dot_nt(wh, xl) + dot_nt(wl, xm))


def folded(x):
    return jnp.concatenate([x[:, j : j + LANES] for j in range(0, x.shape[1], LANES)], axis=0)


def unfolded(x):
    return jnp.concatenate([x[j : j + 8, :] for j in range(0, x.shape[0], 8)], axis=1)


def opening_kernel(zeros_ref):
    zeros_ref[...] = jnp.zeros(zeros_ref.shape, F32)


def lines_kernel(areas, regions, near, zeros_ref, idx_ref, active_ref, count_ref, zone_ref, block_ref, own_ref, weight_ref):
    slots, _, lines = idx_ref.shape
    pieces = lines // LANES
    numbers = jnp.where(active_ref[...] > 0, count_ref[...], 0).astype(F32)

    def idx_row(p, j):
        return idx_ref[p, :, pl.ds(j * LANES, LANES)].astype(F32)

    block_ref[pl.ds(block_ref.shape[0] - 8, 8), :] = zeros_ref[...]
    for p in range(slots):
        for j in range(pieces):
            block_ref[pl.ds(p * pieces + j, 1), :] = idx_row(p, j)
    block_ref[pl.ds(slots * pieces, 1), :] = jnp.full((1, LANES), zone_ref[0].astype(F32))
    block_ref[pl.ds(slots * pieces + 1, 1), pl.ds(0, slots)] = numbers
    weight_ref[...] = line_tables(
        areas, regions, slots, pieces, near, idx_row, lambda p: numbers[:, p : p + 1], own_ref, weight_ref.shape[0]
    )


def first_kernel(slots, pieces, k_ref, load_ref, cap_ref, block_ref, edge_ref, *refs):
    *lean_refs, rest_ref, v_ref, lin_ref, kh_ref, kl_ref, over_ref = refs
    scens = lin_ref.shape[0]
    edge_ref[pl.ds(scens, block_ref.shape[0]), :] = block_ref[...]
    for ref, p in zip(lean_refs, (2, 4)):
        ref[pl.ds(scens, 2 * pieces), :] = block_ref[pl.ds(p * pieces, 2 * pieces), :]
        rest = ref.shape[0] - scens - 2 * pieces
        ref[pl.ds(scens + 2 * pieces, rest), :] = jnp.broadcast_to(
            block_ref[pl.ds(slots * pieces, 1), :], (rest, LANES)
        )
    high, low = halves(k_ref[0].T)
    kh_ref[...] = high
    kl_ref[...] = low
    lin_ref[...] = load_ref[0].T
    limits = cap_ref[...]

    def start(rows):
        return lin_ref[rows, :], jnp.zeros((CHAIN_ROWS, lin_ref.shape[1]), F32)

    def finish(rows, x, over):
        for ref in (edge_ref, *lean_refs):
            ref[rows, :] = x[:, :BOUNDARY]
        rest_ref[rows, :] = x[:, BOUNDARY:]
        v_ref[rows, :] = x + over

    run_sweeps(start, finish, lin_ref, over_ref, limits, kh_ref, kl_ref, INNER)


def share_kernel(areas, regions, near, zone_at, weight_ref, edge_ref, rest_ref, share_ref, *across_refs):
    scens = rest_ref.shape[0]
    x = jnp.concatenate([edge_ref[pl.ds(0, scens), :], rest_ref[...]], axis=1)
    sums = weighted_sums(weight_ref[...], x)
    if near:
        share_ref[...] = folded(sums[0:8, :])
        row_id = lax.broadcasted_iota(jnp.int32, (8, scens), 0)
        across = jnp.where(row_id == lax.axis_index("area"), sums[areas + 1 : areas + 2, :], 0.0)
        across_refs[0][...] = folded(jnp.where(row_id == areas, sums[areas : areas + 1, :], across))
        return
    if zone_at is not None:
        me = lax.axis_index("area") * regions + lax.axis_index("region")
        zone = edge_ref[pl.ds(zone_at, 1), pl.ds(0, 1)]
        row_id = lax.broadcasted_iota(jnp.int32, sums.shape, 0)
        sums = sums + jnp.where(row_id == areas * regions + 1 + me, zone, 0.0)
    share_ref[...] = sums[0 : share_ref.shape[0], :]


def append_kernel(scens, kept, zone_at, share_ref, across_ref, edge_ref, pair_ref, full_ref):
    pair = share_ref[...] + across_ref[...]
    rows = pair.shape[0]
    pair_ref[...] = pair
    full_ref[pl.ds(0, scens), :] = edge_ref[pl.ds(0, scens), :]
    full_ref[pl.ds(scens, rows), :] = pair
    full_ref[pl.ds(scens + rows, kept), :] = edge_ref[pl.ds(scens, kept), :]
    full_ref[pl.ds(scens + rows + kept, 1), :] = edge_ref[pl.ds(zone_at, 1), :]


def live_lines(edge_ref, scens, slots, pieces, p):
    return edge_ref[pl.ds(scens + slots * pieces + 1, 1), pl.ds(p, 1)]


def by_area(values):
    me = lax.axis_index("area")
    out = []
    for k in range(4):
        mask = jnp.bitwise_xor(me, k)
        low = jnp.where(jnp.bitwise_and(mask, 1) == 0, values[0], values[1])
        high = jnp.where(jnp.bitwise_and(mask, 1) == 0, values[2], values[3])
        out.append(jnp.where(mask < 2, low, high))
    return out


def near_sums(scens, pair_ref, opposite_ref, far_ref, close_ref):
    rows = pl.ds(scens, pair_ref.shape[0])
    return unfolded((pair_ref[...] + close_ref[rows, :]) + (opposite_ref[...] + far_ref[rows, :]))


def near_prices(sums, zones, zone):
    price = sums[4:5, :] * SYSTEM_GAIN
    for k in range(4):
        price = price + jnp.where(zones[k] == zone, ZONE_GAIN, 0.0) * sums[k : k + 1, :]
    return price


def prices(shares, zones, total, regions, zone):
    ids = lax.broadcasted_iota(jnp.int32, zones.shape, 0)
    in_region = lax.rem(ids, regions) == lax.axis_index("region")
    gain = jnp.where(in_region & (zones == zone), ZONE_GAIN, 0.0) + SYSTEM_GAIN
    return jnp.sum(gain * shares[0:total, :], axis=0, keepdims=True)


class Mask(int):
    pass


class Plan:
    def __init__(self, areas, regions, scens, slots, pieces):
        self.near = (areas, regions) == (4, 2)
        self.scens, self.pieces = scens, pieces
        self.fold = 8 * (scens // LANES)
        if self.near:
            self.sources = [("area", Mask(2)), ("area", Mask(3)), ("area", Mask(1)), ("region", 1)]
            self.slots_of = [(2, 3), ((1, 0),), ((0, 1),), (4, 5)]
            self.buffer_of = [(2, 1), (1, 2), 0, 0, 3, 3]
            self.arrivals = [(0,), (3,), (1, 2)]
            self.last = (1, 2, 3)
            return
        self.sources, self.slots_of, self.buffer_of = [], [], [None] * slots
        for p in (2, 3, 0, 1, 4, 5):
            axis, move, _ = SLOTS[p]
            source = (axis, move % (areas if axis == "area" else regions))
            if source not in self.sources:
                self.sources.append(source)
                self.slots_of.append(())
            self.buffer_of[p] = self.sources.index(source)
            self.slots_of[self.buffer_of[p]] += (p,)
        self.arrivals = [tuple(range(len(self.sources)))]
        self.last = self.arrivals[0]

    def line_row(self, b, p, j):
        back = SLOTS[p][2]
        if self.near:
            back -= {0: 2, 3: 4}.get(b, 0)
        return self.scens + (self.fold if self.near and b in (1, 2) else 0) + back * self.pieces + j

    def zone_row(self, b):
        return self.scens + (self.fold if b in (1, 2) else 0) + 2 * self.pieces


def choice(entry, read):
    if isinstance(entry, int):
        return read(entry)
    even = lax.rem(lax.axis_index("area"), 2) == 0
    return jnp.where(even, read(entry[0]), read(entry[1]))


def coupling_kernel(plan, held, own_ref, *refs):
    got, before, coupling_ref = refs[: len(held)], refs[len(held) : -1], refs[-1]
    lines = plan.pieces * LANES
    bus_id = lax.broadcasted_iota(jnp.int32, (BOUNDARY, LANES), 0).astype(F32)
    counts = []
    for b, g in zip(held, got):
        met = None
        for entry in plan.slots_of[b]:
            mine = choice(entry, lambda p: own_ref[:, pl.ds(p * lines, lines)])
            there = []
            for j in range(plan.pieces):
                row = choice(entry, lambda p: g[pl.ds(plan.line_row(b, p, j), 1), :])
                there.append(jnp.where(bus_id == row, 1.0, 0.0).astype(BF16))
            pairs = dot_nt(mine, jnp.concatenate(there, axis=1))
            met = pairs if met is None else met + pairs
        counts.append(met)
    counts_high, counts_low = halves(jnp.concatenate(counts, axis=1))
    high, low = halves(jnp.concatenate([g[pl.ds(0, plan.scens), :] for g in got], axis=1))
    out = dot_nt(high, counts_high) + dot_nt(low, counts_high) + dot_nt(high, counts_low)
    for ref in before:
        out = out + ref[...]
    coupling_ref[...] = out


def second_kernel(
    areas, regions, plan, zone_at, *refs
):
    *front, lin_ref, coupling_ref, v_ref, kh_ref, kl_ref, cap_ref, edge1_ref = refs[:-6]
    refs = (*front, *refs[-6:])
    edge_ref, rest_ref, sums_ref, lin2_ref, over_ref = refs[-5:]
    scens = lin_ref.shape[0]
    zone = edge1_ref[pl.ds(zone_at, 1), pl.ds(0, 1)]
    if plan.near:
        pair_ref, opposite_ref, *got = refs[:-6]
        sums = near_sums(scens, pair_ref, opposite_ref, got[1], got[2])
        zones = by_area([zone] + [got[b][pl.ds(plan.zone_row(b), 1), pl.ds(0, 1)] for b in (2, 0, 1)])
        price = near_prices(sums, zones, zone)
        sums_ref[pl.ds(0, 8), :] = sums
        sums_ref[pl.ds(8, 8), :] = jnp.zeros((8, scens), F32)
        for k in range(4):
            sums_ref[pl.ds(8 + k, 1), :] = jnp.broadcast_to(zones[k], (1, scens))
    else:
        total = areas * regions
        sums = refs[0][...]
        sums_ref[...] = sums
        price = prices(sums, sums[total + 1 : 2 * total + 1, :], total, regions, zone)
    price = jnp.broadcast_to(price, (8, scens)).T[:, 0:1]
    lin2_ref[:, pl.ds(0, BOUNDARY)] = lin_ref[:, pl.ds(0, BOUNDARY)] - price - coupling_ref[...]
    lin2_ref[:, pl.ds(BOUNDARY, BOUNDARY)] = lin_ref[:, pl.ds(BOUNDARY, BOUNDARY)] - price
    limits = cap_ref[...]

    def start(rows):
        clipped, over = clipping(v_ref[rows, :], limits)
        return lin2_ref[rows, :] + (clipped - over), over

    def finish(rows, x, over):
        edge_ref[rows, :] = x[:, :BOUNDARY]
        rest_ref[rows, :] = x[:, BOUNDARY:]

    run_sweeps(start, finish, lin2_ref, over_ref, limits, kh_ref, kl_ref, INNER)


def injection_kernel(edge_ref, rest_ref, injection_ref):
    scens = rest_ref.shape[0]
    injection_ref[0, pl.ds(0, BOUNDARY), :] = edge_ref[pl.ds(0, scens), :].T
    injection_ref[0, pl.ds(BOUNDARY, BOUNDARY), :] = rest_ref[...].T


def own_table_kernel(plan, own_ref, table_ref):
    pieces, scens = plan.pieces, plan.scens
    mine = own_ref[pl.ds(scens, own_ref.shape[0] - scens), :].T
    fill_table(plan, own_ref, table_ref, 0.5, lambda p, j: mine[:, p * pieces + j : p * pieces + j + 1])


def fill_table(plan, own_ref, table_ref, half, column):
    slots, pieces, scens = table_ref.shape[0], plan.pieces, plan.scens
    bus_id = lax.broadcasted_iota(jnp.int32, (LANES, BOUNDARY), 1).astype(F32)
    line_id = lax.broadcasted_iota(jnp.int32, (LANES, BOUNDARY), 0).astype(F32)
    for p in range(slots):
        number = live_lines(own_ref, scens, slots, pieces, p)
        for j in range(pieces):
            live = jnp.where(line_id + float(j * LANES) < number, half * SIGNS[p], 0.0)
            table_ref[p, pl.ds(j * LANES, LANES), :] = jnp.where(bus_id == column(p, j), live, 0.0).astype(BF16)


def table_kernel(plan, own_ref, *refs):
    got = refs[:-1]
    table_ref = refs[-1]
    slots, pieces = table_ref.shape[0], plan.pieces
    rows = []
    for p in range(slots):
        rows += [choice(plan.buffer_of[p], lambda b: got[b][pl.ds(plan.line_row(b, p, j), 1), :]) for j in range(pieces)]
        rows.append(jnp.zeros((8 - pieces, LANES), F32))
    theirs = jnp.concatenate(rows, axis=0).T
    fill_table(plan, own_ref, table_ref, -0.5, lambda p, j: theirs[:, p * 8 + j : p * 8 + j + 1])


def twice(x):
    return jnp.concatenate([x, x], axis=1)


def own_kernel(table_ref, edge_ref, flow_ref):
    scens = flow_ref.shape[2]
    parts = jnp.concatenate(halves(edge_ref[pl.ds(0, scens), :]), axis=1)
    for p in range(table_ref.shape[0]):
        flow_ref[p] = dot_nt(twice(table_ref[p]), parts)


def write_flows(plan, held, parts, table_ref, own_ref, flow_ref, flow_hbm, sems):
    copies = []
    for i, p in enumerate(held):
        part = choice(plan.buffer_of[p], lambda b: parts[b])
        flow_ref[i] = own_ref[p] + dot_nt(twice(table_ref[p]), part)
        copies.append(pltpu.make_async_copy(flow_ref.at[i], flow_hbm.at[0, p], sems.at[i]))
        copies[-1].start()
    return copies


def parts_of(plan, refs, held):
    return {b: jnp.concatenate(halves(ref[pl.ds(0, plan.scens), :]), axis=1) for b, ref in zip(held, refs)}


def parts_kernel(ref, part_ref):
    part_ref[...] = jnp.concatenate(halves(ref[pl.ds(0, part_ref.shape[0]), :]), axis=1)


def final_kernel(plan, table_ref, own_ref, *refs):
    *got, flow_hbm, done_ref, flow_ref, sems = refs
    if plan.near:
        parts = {0: got[0][...]}
        got = got[1:]
    else:
        parts = {}
    parts.update(parts_of(plan, got, plan.last))
    copies = write_flows(plan, (2, 3, 4, 5, 0, 1), parts, table_ref, own_ref, flow_ref, flow_hbm, sems)
    done_ref[...] = jnp.zeros(done_ref.shape, F32)
    for copy in copies:
        copy.wait()


def price_kernel(areas, regions, near, first_ref, done_ref, *refs):
    *rest, price_ref = refs
    if near:
        own, two, one, three = rest
        sums = first_ref[pl.ds(0, 8), :] + unfolded((own[...] + one[...]) + (two[...] + three[...]))
        zones = [first_ref[pl.ds(8 + k, 1), :] for k in range(4)]
        for z in range(ZONES):
            price_ref[pl.ds(z, 1), :] = near_prices(sums, zones, float(z))
        return
    total = areas * regions
    first = first_ref[...]
    zones = first[total + 1 : 2 * total + 1, :]
    for z in range(ZONES):
        price_ref[pl.ds(z, 1), :] = prices(first + rest[0][...], zones, total, regions, float(z))


def moved(x, axis, by):
    length = lax.axis_size(axis)
    if isinstance(by, Mask):
        return lax.ppermute(x, axis, [(i, i ^ by) for i in range(length)])
    return lax.ppermute(x, axis, [((i + by) % length, i) for i in range(length)])


def body(kkt_inverse, scen_load, capacity, pair_active, tie_counts, line_index, area_zone):
    areas = lax.axis_size("area")
    regions = lax.axis_size("region")
    total = areas * regions
    _, buses, scens = scen_load.shape
    _, slots, lines = line_index.shape
    rest = buses - BOUNDARY
    pieces = lines // LANES
    plan = Plan(areas, regions, scens, slots, pieces)
    near = plan.near
    zone_at = scens + slots * pieces
    share_rows = -(-(2 * total + 1) // 8) * 8
    weight_rows = 16 if near else -(-share_rows // 16) * 16

    def f32(*shape):
        return jax.ShapeDtypeStruct(shape, F32)

    def bf16(*shape):
        return jax.ShapeDtypeStruct(shape, BF16)

    def cost(flops):
        return pl.CostEstimate(flops=flops, bytes_accessed=0, transcendentals=0)

    def call(kernel, name, out_shape, operands, estimate=None, **more):
        return pl.pallas_call(
            kernel,
            out_shape=out_shape,
            in_specs=more.pop("in_specs", [VMEM] * len(operands)),
            out_specs=more.pop("out_specs", jax.tree.map(lambda _: VMEM, out_shape)),
            compiler_params=PARAMS,
            cost_estimate=estimate and cost(estimate),
            name=name,
            **more,
        )(*operands)

    def exchange_last(edge, rest, weights):
        got = [moved(edge, axis, move) for axis, move in plan.sources[::-1]][::-1]
        share, across = call(
            functools.partial(share_kernel, areas, regions, near, None),
            "mismatch_shares",
            [f32(plan.fold, LANES)] * 2,
            [weights, edge, rest],
        )
        pair = share + moved(across, "region", 1)
        return got, [pair, *(moved(pair, "area", Mask(mask)) for mask in (2, 1, 3))]

    def exchange(edge, rest, leans, weights, kept):
        held = edge.shape[0] > scens
        shapes = [f32(plan.fold, LANES)] * 2 if near else [f32(share_rows, scens)]
        share, *across = call(
            functools.partial(share_kernel, areas, regions, near, zone_at if held else None),
            "mismatch_shares",
            shapes,
            [weights, edge, rest],
        )
        if not near:
            return [moved(edge, axis, move) for axis, move in plan.sources], [lax.psum(share, ("area", "region"))]
        far, side = leans
        pair, full = call(
            functools.partial(append_kernel, scens, kept, zone_at),
            "pair_shares",
            [f32(plan.fold, LANES), f32(scens + plan.fold + -(-(kept + 1) // 8) * 8, BOUNDARY)],
            [share, moved(across[0], "region", 1), edge],
        )
        got = [moved(x, *source) for x, source in zip((far, full, full, side), plan.sources)]
        return got, [pair, moved(pair, "area", Mask(2))]

    zeros = call(opening_kernel, "opening", f32(8, LANES), [], OPENING)
    lean_rows = -(-(scens + 2 * pieces + 1) // 8) * 8
    leans = [f32(lean_rows, BOUNDARY)] * 2 if near else []
    block, own, weights = call(
        functools.partial(lines_kernel, areas, regions, near),
        "line_blocks",
        [
            f32(-(-(slots * pieces + 2) // 8) * 8, LANES),
            bf16(BOUNDARY, slots * lines),
            f32(weight_rows, buses),
        ],
        [zeros, line_index.reshape(slots, 1, lines), pair_active, tie_counts, area_zone],
        in_specs=[VMEM] * 4 + [SMEM],
    )
    edge1, *more = call(
        functools.partial(first_kernel, slots, pieces),
        "first_round",
        [
            f32(scens + block.shape[0], BOUNDARY),
            *leans,
            f32(scens, rest),
            f32(scens, buses),
            f32(scens, buses),
            bf16(buses, buses),
            bf16(buses, buses),
        ],
        [kkt_inverse, scen_load, capacity, block],
        scratch_shapes=[pltpu.VMEM((scens, buses), F32)],
    )
    leans1, (rest1, state, lin, kh, kl) = more[: len(leans)], more[len(leans) :]
    got1, sums1 = exchange(edge1, rest1, leans1, weights, 2 * pieces)
    coupling = []
    for held in plan.arrivals:
        coupling = [
            call(
                functools.partial(coupling_kernel, plan, held),
                "coupling",
                f32(scens, BOUNDARY),
                [own, *(got1[b] for b in held), *coupling],
                BIG,
            )
        ]
    mine = call(functools.partial(own_table_kernel, plan), "own_table", bf16(slots, lines, BOUNDARY), [edge1])
    edge2, rest2, first = call(
        functools.partial(second_kernel, areas, regions, plan, zone_at),
        "second_round",
        [f32(scens, BOUNDARY), f32(scens, rest), f32(16 if near else share_rows, scens)],
        [*sums1, *(got1 if near else []), lin, *coupling, state, kh, kl, capacity, edge1, mine],
        scratch_shapes=[pltpu.VMEM((scens, buses), F32)] * 2,
    )
    if near:
        got2, sums2 = exchange_last(edge2, rest2, weights)
    else:
        got2, sums2 = exchange(edge2, rest2, [], weights, 0)
    injection = call(injection_kernel, "injection", f32(1, buses, scens), [edge2, rest2])
    theirs = call(functools.partial(table_kernel, plan), "line_table", bf16(slots, lines, BOUNDARY), [edge1, *got1])
    own_flow = call(own_kernel, "own_flows", f32(slots, lines, scens), [mine, edge2])
    operands = got2
    if near:
        far = call(parts_kernel, "injection_parts", bf16(scens, 2 * BOUNDARY), got2[:1], BIG)
        operands = [far, *(got2[b] for b in plan.last)]
    flow, done = call(
        functools.partial(final_kernel, plan),
        "tie_flows",
        (f32(1, slots, lines, scens), f32(8, LANES)),
        [theirs, own_flow, *operands],
        BIG,
        out_specs=(HBM, VMEM),
        scratch_shapes=[pltpu.VMEM((slots, lines, scens), F32), pltpu.SemaphoreType.DMA((slots,))],
    )
    price = call(
        functools.partial(price_kernel, areas, regions, near),
        "zone_prices",
        f32(ZONES, scens),
        [first, done, *sums2],
    )
    return injection, flow, price


def solution(mesh):
    placed = (
        P(("area", "region"), None, None),
        P(("area", "region"), None, ("group", "scen")),
        P(("area", "region"), None),
        P(("area", "region"), None),
        P(("area", "region"), None),
        P(("area", "region"), None, None),
        P(("area", "region")),
    )
    return jax.shard_map(
        body,
        mesh=mesh,
        in_specs=placed,
        out_specs=(
            P(("area", "region"), None, ("group", "scen")),
            P(("area", "region"), None, None, ("group", "scen")),
            P("region", ("group", "scen")),
        ),
        check_vma=False,
    )
```
